32 devices in a mesh: seq: 8 (over z, y), tp: 4 (over x, core).
Axes of the slice: x: 2, y: 2, z: 4, core: 2. Of those that a mesh axis runs over, the one named last changes fastest.
Arguments:
- queries: bfloat16 [2048, 8192], P('seq', 'tp'), may hold values from -6 to 6
- key_matrix: bfloat16 [2048, 1024], P('seq', 'tp'), may hold values from -6 to 6
- value_matrix: bfloat16 [2048, 1024], P('seq', 'tp'), may hold values from -6 to 6
- output_gradient: bfloat16 [2048, 8192], P(('seq', 'tp')), may hold values from -6 to 6
- document: int32 [2048], P('seq'), may hold values from 0 to 7, never falling along the last dimension, each value on 1 to 1024 neighbouring positions
Outputs:
- query_grad: bfloat16 [2048, 8192], P('seq', 'tp')
- key_gradient: bfloat16 [2048, 1024], P('seq', 'tp')
- value_gradient: bfloat16 [2048, 1024], P('seq', 'tp')
The draws below stay inside these ranges and needn't reach their ends.
Inputs may be any that keep to these rules, and one draw needn't show every extreme that they name: document never falls along the sequence; there are exactly 8 documents, each of at most 1024 tokens, and one holds exactly that many.
All inputs are finite; a program needn't handle non-finite values.
Results may differ from the reference program's by a relative error of at most 0.009.
Values may be sent and summed in bfloat16 or wider, within the bound.
No kernel may reach another device: no remote copies, remote signals or barrier semaphores. Data moves between devices by JAX's collectives and lax.ppermute only.
A program may use at most 64 MiB of HBM per device.

```python
import math
import jax
import jax.numpy as jnp
import numpy as np
from jax import lax

QUERY_HEADS = 64
KEY_VALUE_HEADS = 8
HEAD_WIDTH = 128
DOCS = 8
WINDOW_TOKENS = 2048


def draw_queries(key, part):
    random_seed_key = jax.random.fold_in(key, 3)
    gaussian_draws = jax.random.normal(random_seed_key, (WINDOW_TOKENS, QUERY_HEADS * HEAD_WIDTH), jnp.float32)
    return jnp.clip(gaussian_draws, -6.0, 6.0).astype(jnp.bfloat16)


def draw_key_matrix(key, part):
    random_seed_key = jax.random.fold_in(key, 5)
    gaussian_draws = jax.random.normal(random_seed_key, (WINDOW_TOKENS, KEY_VALUE_HEADS * HEAD_WIDTH), jnp.float32)
    return jnp.clip(gaussian_draws, -6.0, 6.0).astype(jnp.bfloat16)


def levels(own_key, shape, pieces, least, top_value):
    def one(position, shards_of):
        steps = jax.random.uniform(jax.random.fold_in(jax.random.fold_in(own_key, 6), position), (shards_of,), jnp.float32, least / len(pieces), top_value / len(pieces))
        return jnp.repeat(jnp.exp(steps), shape[position] // shards_of).reshape((-1,) + (1,) * (len(shape) - position - 1))

    loudness = one(*pieces[0])
    for cut in pieces[1:]:
        loudness = loudness * one(*cut)
    return loudness


def length_profile(count, total, bound, slope):
    weights = [(1 << 20) // math.isqrt(grade ** slope) + 1 for grade in range(2, count + 1)]
    surplus, holding = total - bound - (count - 1), [1] * (count - 1)
    while surplus > 0:
        free = [i for i in range(count - 1) if holding[i] < bound]
        whole, left = sum([weights[i] for i in free]), surplus
        for i in free:
            addition = min(bound - holding[i], max(1, left * weights[i] // whole), surplus)
            holding[i] = holding[i] + addition
            surplus = surplus - addition
    return np.array([bound] + holding)


def ragged(own_key, amount, total, bound, slope):
    if amount == 2:
        one = jax.random.randint(own_key, (), max(1, total - bound), min(bound, total - 1) + 1)
        return jnp.stack([one, total - one])
    sizes = jnp.asarray(length_profile(amount, total, bound, slope), jnp.int32)
    twos = (amount - 1) // 2
    donor, sink = sizes[1:1 + 2 * twos:2], sizes[2:2 + 2 * twos:2]
    slack = jnp.minimum(donor - 1, bound - sink)
    shifted = jax.random.randint(jax.random.fold_in(own_key, 1), (twos,), 0, 1 << 20) % (slack + 1)
    sizes = sizes.at[1:1 + 2 * twos:2].set(donor - shifted).at[2:2 + 2 * twos:2].set(sink + shifted)
    return sizes[jax.random.permutation(jax.random.fold_in(own_key, 2), amount)]


def normal_values(key, extent, width, bound, pieces=(), held_as=jnp.bfloat16):
    drawn = width * jax.random.normal(key, extent, jnp.float32)
    if pieces:
        drawn = drawn * levels(key, extent, pieces, -0.22, 0.18)
    return jnp.clip(drawn, -bound, bound).astype(held_as)


def setup_inputs(seed: int = 0) -> dict:
    seeds = jax.random.split(jax.random.key(seed), 6)
    return {
        "queries": draw_queries(jax.random.fold_in(seeds[5], 71), 0),
        "key_matrix": draw_key_matrix(jax.random.fold_in(seeds[5], 71), 0),
        "value_matrix": normal_values(seeds[2], (WINDOW_TOKENS, KEY_VALUE_HEADS * HEAD_WIDTH), 1.0, 6.0, ((0, 8), (1, 4))),
        "output_gradient": normal_values(seeds[3], (WINDOW_TOKENS, QUERY_HEADS * HEAD_WIDTH), 1.0, 6.0, ((0, 32),)),
        "document": jnp.searchsorted(jnp.cumsum(ragged(seeds[4], DOCS, WINDOW_TOKENS, WINDOW_TOKENS // 2, 2)), jnp.arange(WINDOW_TOKENS), side="right").astype(jnp.int32),
    }


neg_big = -1e+30

def reference(queries, key_matrix, value_matrix, output_gradient, document):
    group_width = QUERY_HEADS // KEY_VALUE_HEADS
    factor = 1.0 / math.sqrt(HEAD_WIDTH)
    query_head_rows = jnp.transpose(queries.reshape(WINDOW_TOKENS, KEY_VALUE_HEADS, group_width, HEAD_WIDTH), (1, 0, 2, 3))
    gradient_heads = jnp.transpose(output_gradient.reshape(WINDOW_TOKENS, KEY_VALUE_HEADS, group_width, HEAD_WIDTH), (1, 0, 2, 3))
    key_head_rows = jnp.transpose(key_matrix.reshape(WINDOW_TOKENS, KEY_VALUE_HEADS, HEAD_WIDTH), (1, 0, 2))
    value_head_rows = jnp.transpose(value_matrix.reshape(WINDOW_TOKENS, KEY_VALUE_HEADS, HEAD_WIDTH), (1, 0, 2))
    rows_blk = math.gcd(WINDOW_TOKENS, 512)
    positions = jnp.arange(WINDOW_TOKENS, dtype=jnp.int32)

    def one_head(operands):
        query_one, grad_one, key_one, value_one = operands
        key_f = key_one.astype(jnp.float32)
        value_f = value_one.astype(jnp.float32)

        def query_block(carry, block_index):
            key_acc, value_acc = carry
            start_row = (block_index * rows_blk).astype(jnp.int32)
            query_blk = lax.dynamic_slice_in_dim(query_one, start_row, rows_blk, 0).astype(jnp.float32)
            grad_blk = lax.dynamic_slice_in_dim(grad_one, start_row, rows_blk, 0).astype(jnp.float32)
            doc_blk = lax.dynamic_slice_in_dim(document, start_row, rows_blk, 0)
            pos_blk = start_row + jnp.arange(rows_blk, dtype=jnp.int32)
            visible = (doc_blk[:, None] == document[None, :]) & (positions[None, :] <= pos_blk[:, None])
            scores = jnp.einsum('igd,jd->gij', query_blk, key_f) * factor
            scores = jnp.where(visible[None], scores, neg_big)
            row_peak = lax.optimization_barrier(jnp.max(scores, axis=-1))
            row_total = lax.optimization_barrier(jnp.sum(jnp.where(visible[None], jnp.exp(scores - row_peak[..., None]), 0.0), axis=-1))
            log_total = row_peak + jnp.log(row_total)
            weights = jnp.where(visible[None], jnp.exp(scores - log_total[..., None]), 0.0)
            weight_grad = jnp.einsum('igd,jd->gij', grad_blk, value_f)
            row_dot = lax.optimization_barrier(jnp.sum(weights * weight_grad, axis=-1))
            weights_half = lax.optimization_barrier(weights.astype(jnp.bfloat16)).astype(jnp.float32)
            score_grad = lax.optimization_barrier((weights * (weight_grad - row_dot[..., None])).astype(jnp.bfloat16)).astype(jnp.float32)
            value_acc = value_acc + jnp.einsum('gij,igd->jd', weights_half, grad_blk)
            key_acc = key_acc + jnp.einsum('gij,igd->jd', score_grad, query_blk)
            query_part = jnp.einsum('gij,jd->igd', score_grad, key_f)
            return ((key_acc, value_acc), query_part)
        zero_keys = jnp.zeros((WINDOW_TOKENS, HEAD_WIDTH), jnp.float32)
        (key_acc, value_acc), query_parts = lax.scan(query_block, (zero_keys, zero_keys), jnp.arange(WINDOW_TOKENS // rows_blk, dtype=jnp.int32))
        query_grad = query_parts.reshape(WINDOW_TOKENS, group_width, HEAD_WIDTH) * factor
        return (query_grad, key_acc * factor, value_acc)
    query_all, key_full, value_full = lax.map(one_head, (query_head_rows, gradient_heads, key_head_rows, value_head_rows))
    query_grad = jnp.transpose(query_all, (1, 0, 2, 3)).reshape(WINDOW_TOKENS, QUERY_HEADS * HEAD_WIDTH).astype(jnp.bfloat16)
    key_gradient = jnp.transpose(key_full, (1, 0, 2)).reshape(WINDOW_TOKENS, KEY_VALUE_HEADS * HEAD_WIDTH).astype(jnp.bfloat16)
    value_gradient = jnp.transpose(value_full, (1, 0, 2)).reshape(WINDOW_TOKENS, KEY_VALUE_HEADS * HEAD_WIDTH).astype(jnp.bfloat16)
    return (query_grad, key_gradient, value_gradient)
```

```python
import functools
import math

import jax
import jax.numpy as jnp
from jax import lax
from jax.experimental import pallas as pl
from jax.experimental.pallas import tpu as pltpu
from jax.sharding import PartitionSpec as P

HEAD_WIDTH = 128
DOCS = 8
PAD = 16
NEG = -1e30
ANY = pl.BlockSpec(memory_space=pl.ANY)


def prep_kernel(n_tp, heads, key_ref, value_ref, doc_ref, grad_ref, *rest):
    kvd_outs, rest = rest[:heads], rest[heads:]
    grad_outs, (sems,) = rest[:-1], rest[-1:]
    tokens = key_ref.shape[0]
    me = lax.axis_index("tp")
    width = grad_ref.shape[1] // n_tp
    part_width = width // heads
    copies = []
    for h in range(heads):
        for part, src in enumerate((key_ref, value_ref)):
            copies.append(
                (
                    src.at[:, pl.ds(h * HEAD_WIDTH, HEAD_WIDTH)],
                    kvd_outs[h].at[pl.ds(0, tokens), pl.ds(part * HEAD_WIDTH, HEAD_WIDTH)],
                )
            )
        for m in range(1, n_tp):
            start = pl.multiple_of((me ^ m) * width + h * part_width, part_width)
            copies.append(
                (grad_ref.at[:, pl.ds(start, part_width)], grad_outs[h * (n_tp - 1) + m - 1])
            )
    started = []
    for index, (src, dst) in enumerate(copies):
        copy = pltpu.make_async_copy(src, dst, sems.at[index])
        copy.start()
        started.append(copy)
    row = doc_ref[...].astype(jnp.float32).astype(jnp.bfloat16)
    for h in range(heads):
        kvd_outs[h][tokens : tokens + PAD, :] = jnp.broadcast_to(row, (PAD, tokens))
    for copy in started:
        copy.wait()


def prep(key_matrix, value_matrix, document, output_gradient, n_tp):
    tokens, kv_width = key_matrix.shape
    rows, grad_width = output_gradient.shape
    heads = kv_width // HEAD_WIDTH
    block = jax.ShapeDtypeStruct((tokens + PAD, 2 * HEAD_WIDTH), jnp.bfloat16)
    chunk = jax.ShapeDtypeStruct((rows, grad_width // (n_tp * heads)), jnp.bfloat16)
    outs = pl.pallas_call(
        functools.partial(prep_kernel, n_tp, heads),
        out_shape=(block,) * heads + (chunk,) * (heads * (n_tp - 1)),
        in_specs=[ANY, ANY, pl.BlockSpec(memory_space=pltpu.VMEM), ANY],
        out_specs=(pl.BlockSpec(memory_space=pltpu.VMEM),) * (heads * n_tp),
        scratch_shapes=[pltpu.SemaphoreType.DMA((heads * (n_tp + 1),))],
    )(key_matrix, value_matrix, document.reshape(1, tokens), output_gradient)
    step = n_tp - 1
    chunks = outs[heads:]
    return outs[:heads], [chunks[h * step : (h + 1) * step] for h in range(heads)]


def after(array, *others):
    return lax.optimization_barrier((array, *others))[0]


def nt_dot(a, b):
    return lax.dot_general(a, b, (((1,), (1,)), ((), ())), preferred_element_type=jnp.float32)


def nn_dot(a, b):
    return lax.dot_general(a, b, (((1,), (0,)), ((), ())), preferred_element_type=jnp.float32)


def main_kernel(h, reach, group, n_tp, first, *refs):
    half = reach // 2
    refs = list(refs)
    take = lambda count: [refs.pop(0) for _ in range(count)]
    (query_ref, own_grad_ref) = take(2)
    grad_refs = take(n_tp - 1)
    (own_ref,) = take(1)
    y_refs = take(half + 1)
    z_refs = [None] + take(half)
    if not first:
        take(1)
    (dq_ref,) = take(1)
    ret_refs = take(reach)
    (own_out_ref,) = take(1)
    (kv, kt, qs, gs, grad_in, query_in, scores, expd, pbuf, dsbuf, dq_acc, ret, own_acc) = take(13)
    (peak, total, weighted, dq_out, sems, out_sems) = take(6)

    T = own_out_ref.shape[0]
    W = group * HEAD_WIDTH
    i = lax.axis_index("seq")
    t = lax.axis_index("tp")
    odd = lax.rem(i, 2)
    g_cols = pl.ds(h * W, W)
    sub = T // n_tp

    def kv_copy(src, d):
        return pltpu.make_async_copy(src, kv.at[reach - d], sems.at[d])

    kv_copy(own_ref, 0).start()
    for k in range(1, half + 1):
        kv_copy(z_refs[k], 2 * k).start()

        @pl.when(odd == 0)
        def _():
            kv_copy(y_refs[k], 2 * k - 1).start()

        @pl.when(odd == 1)
        def _():
            kv_copy(y_refs[k - 1], 2 * k - 1).start()

    base = reach + 1
    q_copy = pltpu.make_async_copy(query_ref.at[:, g_cols], query_in, sems.at[base])
    q_copy.start()
    g_copies = []
    for m in range(n_tp):
        rows = pl.ds(pl.multiple_of((t ^ m) * sub, sub), sub)
        if m == 0:
            start = pl.multiple_of(t * (own_grad_ref.shape[1] // n_tp) + h * W, W)
            src = own_grad_ref.at[:, pl.ds(start, W)]
        else:
            src = grad_refs[m - 1]
        copy = pltpu.make_async_copy(src, grad_in.at[rows, :], sems.at[base + 1 + m])
        copy.start()
        g_copies.append(copy)

    q_copy.wait()
    for g in range(group):
        qs[pl.ds(g * T, T), :] = query_in[:, g * HEAD_WIDTH : (g + 1) * HEAD_WIDTH]
    for d in range(reach + 1):
        kv_copy(own_ref, d).wait()

    doc_own = kv[reach, T : T + 1, :].astype(jnp.float32)
    held = [jnp.zeros_like(doc_own) for _ in range(DOCS)]
    for d in range(reach + 1):
        row = kv[reach - d, T : T + 1, :].astype(jnp.float32)
        row = jnp.where(i >= d, row, -1.0)
        for u in range(-1, DOCS - 1):
            held[u + 1] = held[u + 1] + jnp.where(row == u, 1.0, 0.0)
    begin = jnp.zeros_like(doc_own)
    for u in range(-1, DOCS - 1):
        count = jnp.sum(held[u + 1], axis=1, keepdims=True)
        begin = begin + jnp.where(doc_own > u, count, 0.0)
    first_key = jnp.min(begin).astype(jnp.int32)
    last_begin = jnp.max(begin).astype(jnp.int32)
    begin = begin.astype(jnp.int32)
    low = first_key // T

    peak[...] = jnp.full(peak.shape, NEG, jnp.float32)
    total[...] = jnp.zeros(total.shape, jnp.float32)
    weighted[...] = jnp.zeros(weighted.shape, jnp.float32)
    dq_acc[...] = jnp.zeros(dq_acc.shape, jnp.float32)

    def score_step(j, _):
        keys = kv[j, 0:T, 0:HEAD_WIDTH]

        def tiles(masked):
            if masked:
                key_pos = j * T + lax.broadcasted_iota(jnp.int32, (T, T), 0)
                query_pos = reach * T + lax.broadcasted_iota(jnp.int32, (T, T), 1)
                seen = (key_pos >= begin) & (key_pos <= query_pos)
            for g in range(group):
                cols = pl.ds(g * T, T)
                s = nt_dot(keys, qs[cols, :])
                if masked:
                    s = jnp.where(seen, s, NEG)
                scores[j, :, cols] = s
                peak[:, cols] = jnp.maximum(
                    peak[:, cols], jnp.max(s.reshape(T // 8, 8, T), axis=0)
                )

        edge = (j * T < last_begin) | (j == reach)
        pl.when(edge)(lambda: tiles(True))
        pl.when(jnp.logical_not(edge))(lambda: tiles(False))
        return 0

    lax.fori_loop(low, reach + 1, score_step, 0)

    for copy in g_copies:
        copy.wait()
    for g in range(group):
        gs[pl.ds(g * T, T), :] = grad_in[:, g * HEAD_WIDTH : (g + 1) * HEAD_WIDTH]

    factor = 1.0 / math.sqrt(HEAD_WIDTH)
    scale = factor * math.log2(math.e)
    top = jnp.max(peak[...], axis=0, keepdims=True) * scale

    def weight_step(j, _):
        values = kv[j, 0:T, HEAD_WIDTH : 2 * HEAD_WIDTH]
        for g in range(group):
            cols = pl.ds(g * T, T)
            e = jnp.exp2(scores[j, :, cols] * scale - top[:, g * T : (g + 1) * T])
            dp = nt_dot(values, gs[cols, :])
            expd[j, :, cols] = e.astype(jnp.bfloat16)
            scores[j, :, cols] = dp
            total[:, cols] += jnp.sum(e.reshape(T // 8, 8, T), axis=0)
            weighted[:, cols] += jnp.sum((e * dp).reshape(T // 8, 8, T), axis=0)
        return 0

    lax.fori_loop(low, reach + 1, weight_step, 0)

    inverse = 1.0 / jnp.sum(total[...], axis=0, keepdims=True)
    row_dot = jnp.sum(weighted[...], axis=0, keepdims=True) * inverse

    def clear_step(j, _):
        ret[j] = jnp.zeros(ret.shape[1:], jnp.bfloat16)
        return 0

    lax.fori_loop(0, low, clear_step, 0)

    def grad_step(j, _):
        keys = kv[j, 0:T, 0:HEAD_WIDTH]
        kt[...] = keys.astype(jnp.float32).T.astype(jnp.bfloat16)
        for g in range(group):
            cols = pl.ds(g * T, T)
            part = slice(g * T, (g + 1) * T)
            p = expd[j, :, cols].astype(jnp.float32) * inverse[:, part]
            ds = (p * (scores[j, :, cols] - row_dot[:, part])).astype(jnp.bfloat16)
            pbuf[:, cols] = p.astype(jnp.bfloat16)
            dsbuf[:, cols] = ds
            dq_acc[:, cols] += nn_dot(kt[...], ds)
        dk = nn_dot(dsbuf[...], qs[...])
        dv = nn_dot(pbuf[...], gs[...])

        @pl.when(j < reach)
        def _():
            ret[j, :, 0:HEAD_WIDTH] = dk.astype(jnp.bfloat16)
            ret[j, :, HEAD_WIDTH : 2 * HEAD_WIDTH] = dv.astype(jnp.bfloat16)

        @pl.when(j == reach)
        def _():
            own_acc[:, 0:HEAD_WIDTH] = dk
            own_acc[:, HEAD_WIDTH : 2 * HEAD_WIDTH] = dv

        return 0

    lax.fori_loop(low, reach + 1, grad_step, 0)

    outs = [pltpu.make_async_copy(own_acc, own_out_ref, out_sems.at[0])]
    for d in range(1, reach + 1):
        outs.append(pltpu.make_async_copy(ret.at[reach - d], ret_refs[d - 1], out_sems.at[d]))
    for copy in outs:
        copy.start()
    for g in range(group):
        piece = (dq_acc[:, g * T : (g + 1) * T] * factor).T
        dq_out[:, g * HEAD_WIDTH : (g + 1) * HEAD_WIDTH] = piece.astype(jnp.bfloat16)
    outs.append(pltpu.make_async_copy(dq_out, dq_ref.at[:, g_cols], out_sems.at[reach + 1]))
    outs[-1].start()
    for copy in outs:
        copy.wait()


def head_call(h, reach, group, n_tp, queries, own_grad, grads, kvd, ys, zs, dq):
    T, q_width = queries.shape
    window = reach + 1
    W = group * HEAD_WIDTH
    first = dq is None
    args = [queries, own_grad, *grads, kvd, *ys, *zs] + ([] if first else [dq])
    flops = 5 * 2 * T * (window * T) * W
    bf16, f32 = jnp.bfloat16, jnp.float32
    outs = pl.pallas_call(
        functools.partial(main_kernel, h, reach, group, n_tp, first),
        out_shape=(jax.ShapeDtypeStruct((T, q_width), bf16),)
        + (jax.ShapeDtypeStruct((T, 2 * HEAD_WIDTH), bf16),) * reach
        + (jax.ShapeDtypeStruct((T, 2 * HEAD_WIDTH), f32),),
        in_specs=[ANY] * len(args),
        out_specs=(ANY,) * (reach + 2),
        input_output_aliases={} if first else {len(args) - 1: 0},
        scratch_shapes=[
            pltpu.VMEM((window, T + PAD, 2 * HEAD_WIDTH), bf16),
            pltpu.VMEM((HEAD_WIDTH, T), bf16),
            pltpu.VMEM((group * T, HEAD_WIDTH), bf16),
            pltpu.VMEM((group * T, HEAD_WIDTH), bf16),
            pltpu.VMEM((T, W), bf16),
            pltpu.VMEM((T, W), bf16),
            pltpu.VMEM((window, T, group * T), f32),
            pltpu.VMEM((window, T, group * T), bf16),
            pltpu.VMEM((T, group * T), bf16),
            pltpu.VMEM((T, group * T), bf16),
            pltpu.VMEM((HEAD_WIDTH, group * T), f32),
            pltpu.VMEM((reach, T, 2 * HEAD_WIDTH), bf16),
            pltpu.VMEM((T, 2 * HEAD_WIDTH), f32),
            pltpu.VMEM((8, group * T), f32),
            pltpu.VMEM((8, group * T), f32),
            pltpu.VMEM((8, group * T), f32),
            pltpu.VMEM((T, W), bf16),
            pltpu.SemaphoreType.DMA((reach + 2 + n_tp,)),
            pltpu.SemaphoreType.DMA((reach + 2,)),
        ],
        compiler_params=pltpu.CompilerParams(vmem_limit_bytes=56 * 1024 * 1024),
        cost_estimate=pl.CostEstimate(
            flops=flops, bytes_accessed=4 * 1024 * 1024, transcendentals=T * window * T * group
        ),
    )(*args)
    return outs[0], outs[1:-1], outs[-1]


def local(queries, key_matrix, value_matrix, output_gradient, document):
    n = lax.axis_size("seq")
    n_tp = lax.axis_size("tp")
    T, q_width = queries.shape
    heads = key_matrix.shape[1] // HEAD_WIDTH
    group = q_width // (heads * HEAD_WIDTH)
    reach = n // 2
    half = reach // 2

    kvds, chunks = prep(key_matrix, value_matrix, document, output_gradient, n_tp)

    swap = [(a, a ^ 1) for a in range(n)]
    rise = [(a, b) for a, b in swap if b > a]
    fall = [(a, b) for a, b in swap if b < a]
    up = [(a, a + 2) for a in range(n - 2)]

    def trade(h, m):
        return lax.ppermute(chunks[h][m - 1], "tp", [(a, a ^ m) for a in range(n_tp)])

    ys = [[lax.ppermute(kvds[h], "seq", rise)] for h in range(heads)]
    zs = [[] for h in range(heads)]
    grads = []
    for h in range(heads):
        level = lax.ppermute(kvds[h], "seq", up)
        far = [trade(h, m) for m in range(2, n_tp)]
        zs[h].append(level)
        for k in range(1, half + 1):
            level = after(level, *far)
            ys[h].append(lax.ppermute(level, "seq", fall if k == half else swap))
            if k < half:
                level = lax.ppermute(level, "seq", up)
                zs[h].append(level)
        grads.append([trade(h, 1)] + far)

    factor = 1.0 / math.sqrt(HEAD_WIDTH)
    dq = None
    keys, values = [], []
    for h in range(heads):
        dq, rets, own = head_call(
            h, reach, group, n_tp, queries, output_gradient, grads[h], kvds[h], ys[h], zs[h], dq
        )
        total = own
        for d in range(reach, 0, -1):
            moved = lax.ppermute(rets[d - 1], "seq", [(a, a - d) for a in range(d, n)])
            total = total + moved.astype(jnp.float32)
        keys.append((total[:, :HEAD_WIDTH] * factor).astype(jnp.bfloat16))
        values.append(total[:, HEAD_WIDTH:].astype(jnp.bfloat16))
    return (dq, jnp.concatenate(keys, axis=1), jnp.concatenate(values, axis=1))


def solution(mesh):
    return jax.shard_map(
        local,
        mesh=mesh,
        in_specs=(P("seq", "tp"), P("seq", "tp"), P("seq", "tp"), P(("seq", "tp"), None), P("seq")),
        out_specs=(P("seq", "tp"), P("seq", "tp"), P("seq", "tp")),
        check_vma=False,
    )
```

```python
import functools
import math

import jax
import jax.numpy as jnp
from jax import lax
from jax.experimental import pallas as pl
from jax.experimental.pallas import tpu as pltpu
from jax.sharding import PartitionSpec as P

HEAD_WIDTH = 128
DOCS = 8
PAD = 16
NEG = -1e30
ANY = pl.BlockSpec(memory_space=pl.ANY)


def prep_kernel(n_tp, heads, key_ref, value_ref, doc_ref, grad_ref, *rest):
    kvd_outs, rest = rest[:heads], rest[heads:]
    grad_outs, (sems,) = rest[:-1], rest[-1:]
    tokens = key_ref.shape[0]
    me = lax.axis_index("tp")
    width = grad_ref.shape[1] // n_tp
    part_width = width // heads
    copies = []
    for h in range(heads):
        for part, src in enumerate((key_ref, value_ref)):
            copies.append(
                (
                    src.at[:, pl.ds(h * HEAD_WIDTH, HEAD_WIDTH)],
                    kvd_outs[h].at[pl.ds(0, tokens), pl.ds(part * HEAD_WIDTH, HEAD_WIDTH)],
                )
            )
        for m in range(1, n_tp):
            start = pl.multiple_of((me ^ m) * width + h * part_width, part_width)
            copies.append(
                (grad_ref.at[:, pl.ds(start, part_width)], grad_outs[h * (n_tp - 1) + m - 1])
            )
    started = []
    for index, (src, dst) in enumerate(copies):
        copy = pltpu.make_async_copy(src, dst, sems.at[index])
        copy.start()
        started.append(copy)
    row = doc_ref[...].astype(jnp.float32).astype(jnp.bfloat16)
    for h in range(heads):
        kvd_outs[h][tokens : tokens + PAD, :] = jnp.broadcast_to(row, (PAD, tokens))
    for copy in started:
        copy.wait()


def prep(key_matrix, value_matrix, document, output_gradient, n_tp):
    tokens, kv_width = key_matrix.shape
    rows, grad_width = output_gradient.shape
    heads = kv_width // HEAD_WIDTH
    block = jax.ShapeDtypeStruct((tokens + PAD, 2 * HEAD_WIDTH), jnp.bfloat16)
    chunk = jax.ShapeDtypeStruct((rows, grad_width // (n_tp * heads)), jnp.bfloat16)
    outs = pl.pallas_call(
        functools.partial(prep_kernel, n_tp, heads),
        out_shape=(block,) * heads + (chunk,) * (heads * (n_tp - 1)),
        in_specs=[ANY, ANY, pl.BlockSpec(memory_space=pltpu.VMEM), ANY],
        out_specs=(pl.BlockSpec(memory_space=pltpu.VMEM),) * (heads * n_tp),
        scratch_shapes=[pltpu.SemaphoreType.DMA((heads * (n_tp + 1),))],
    )(key_matrix, value_matrix, document.reshape(1, tokens), output_gradient)
    step = n_tp - 1
    chunks = outs[heads:]
    return outs[:heads], [chunks[h * step : (h + 1) * step] for h in range(heads)]


def after(array, *others):
    return lax.optimization_barrier((array, *others))[0]


def nt_dot(a, b):
    return lax.dot_general(a, b, (((1,), (1,)), ((), ())), preferred_element_type=jnp.float32)


def nn_dot(a, b):
    return lax.dot_general(a, b, (((1,), (0,)), ((), ())), preferred_element_type=jnp.float32)


def main_kernel(h, reach, group, n_tp, first, *refs):
    half = reach // 2
    refs = list(refs)
    take = lambda count: [refs.pop(0) for _ in range(count)]
    (query_ref, own_grad_ref) = take(2)
    grad_refs = take(n_tp - 1)
    (own_ref,) = take(1)
    (jump_ref,) = take(1)
    y_refs = [None] + take(half - 1)
    z_refs = [None] + take(half)
    if not first:
        take(1)
    (dq_ref,) = take(1)
    (jump_out,) = take(1)
    y_outs = [None] + take(half - 1)
    z_outs = [None] + take(half)
    (own_out_ref,) = take(1)
    (kv, kt, qs, gs, grad_in, query_in, scores, expd, pbuf, dsbuf, dq_acc, ret, own_acc) = take(13)
    (peak, total, weighted, dq_out, sems, out_sems) = take(6)

    T = own_out_ref.shape[0]
    W = group * HEAD_WIDTH
    i = lax.axis_index("seq")
    t = lax.axis_index("tp")
    odd = lax.rem(i, 2)
    g_cols = pl.ds(h * W, W)
    sub = T // n_tp

    def kv_copy(src, d):
        return pltpu.make_async_copy(src, kv.at[reach - d], sems.at[d])

    kv_copy(own_ref, 0).start()
    kv_copy(jump_ref, jnp.where(odd == 1, 1, reach - 1)).start()
    for k in range(1, half + 1):
        kv_copy(z_refs[k], 2 * k).start()
        if k < half:
            kv_copy(y_refs[k], 2 * k - 1 + 2 * odd).start()

    base = reach + 1
    q_copy = pltpu.make_async_copy(query_ref.at[:, g_cols], query_in, sems.at[base])
    q_copy.start()
    g_copies = []
    for m in range(n_tp):
        rows = pl.ds(pl.multiple_of((t ^ m) * sub, sub), sub)
        if m == 0:
            start = pl.multiple_of(t * (own_grad_ref.shape[1] // n_tp) + h * W, W)
            src = own_grad_ref.at[:, pl.ds(start, W)]
        else:
            src = grad_refs[m - 1]
        copy = pltpu.make_async_copy(src, grad_in.at[rows, :], sems.at[base + 1 + m])
        copy.start()
        g_copies.append(copy)

    q_copy.wait()
    for g in range(group):
        qs[pl.ds(g * T, T), :] = query_in[:, g * HEAD_WIDTH : (g + 1) * HEAD_WIDTH]
    for d in range(reach + 1):
        kv_copy(own_ref, d).wait()

    doc_own = kv[reach, T : T + 1, :].astype(jnp.float32)
    held = [jnp.zeros_like(doc_own) for _ in range(DOCS)]
    for d in range(reach + 1):
        row = kv[reach - d, T : T + 1, :].astype(jnp.float32)
        row = jnp.where(i >= d, row, -1.0)
        for u in range(-1, DOCS - 1):
            held[u + 1] = held[u + 1] + jnp.where(row == u, 1.0, 0.0)
    begin = jnp.zeros_like(doc_own)
    for u in range(-1, DOCS - 1):
        count = jnp.sum(held[u + 1], axis=1, keepdims=True)
        begin = begin + jnp.where(doc_own > u, count, 0.0)
    first_key = jnp.min(begin).astype(jnp.int32)
    last_begin = jnp.max(begin).astype(jnp.int32)
    begin = begin.astype(jnp.int32)
    low = first_key // T

    peak[...] = jnp.full(peak.shape, NEG, jnp.float32)
    total[...] = jnp.zeros(total.shape, jnp.float32)
    weighted[...] = jnp.zeros(weighted.shape, jnp.float32)
    dq_acc[...] = jnp.zeros(dq_acc.shape, jnp.float32)

    def score_step(j, _):
        keys = kv[j, 0:T, 0:HEAD_WIDTH]

        def tiles(masked):
            if masked:
                key_pos = j * T + lax.broadcasted_iota(jnp.int32, (T, T), 0)
                query_pos = reach * T + lax.broadcasted_iota(jnp.int32, (T, T), 1)
                seen = (key_pos >= begin) & (key_pos <= query_pos)
            for g in range(group):
                cols = pl.ds(g * T, T)
                s = nt_dot(keys, qs[cols, :])
                if masked:
                    s = jnp.where(seen, s, NEG)
                scores[j, :, cols] = s
                peak[:, cols] = jnp.maximum(
                    peak[:, cols], jnp.max(s.reshape(T // 8, 8, T), axis=0)
                )

        edge = (j * T < last_begin) | (j == reach)
        pl.when(edge)(lambda: tiles(True))
        pl.when(jnp.logical_not(edge))(lambda: tiles(False))
        return 0

    lax.fori_loop(low, reach + 1, score_step, 0)

    for copy in g_copies:
        copy.wait()
    for g in range(group):
        gs[pl.ds(g * T, T), :] = grad_in[:, g * HEAD_WIDTH : (g + 1) * HEAD_WIDTH]

    factor = 1.0 / math.sqrt(HEAD_WIDTH)
    scale = factor * math.log2(math.e)
    top = jnp.max(peak[...], axis=0, keepdims=True) * scale

    def weight_step(j, _):
        values = kv[j, 0:T, HEAD_WIDTH : 2 * HEAD_WIDTH]
        for g in range(group):
            cols = pl.ds(g * T, T)
            e = jnp.exp2(scores[j, :, cols] * scale - top[:, g * T : (g + 1) * T])
            dp = nt_dot(values, gs[cols, :])
            expd[j, :, cols] = e.astype(jnp.bfloat16)
            scores[j, :, cols] = dp
            total[:, cols] += jnp.sum(e.reshape(T // 8, 8, T), axis=0)
            weighted[:, cols] += jnp.sum((e * dp).reshape(T // 8, 8, T), axis=0)
        return 0

    lax.fori_loop(low, reach + 1, weight_step, 0)

    inverse = 1.0 / jnp.sum(total[...], axis=0, keepdims=True)
    row_dot = jnp.sum(weighted[...], axis=0, keepdims=True) * inverse

    def clear_step(j, _):
        ret[j] = jnp.zeros(ret.shape[1:], jnp.bfloat16)
        return 0

    lax.fori_loop(0, low, clear_step, 0)

    def grad_step(j, _):
        keys = kv[j, 0:T, 0:HEAD_WIDTH]
        kt[...] = keys.astype(jnp.float32).T.astype(jnp.bfloat16)
        for g in range(group):
            cols = pl.ds(g * T, T)
            part = slice(g * T, (g + 1) * T)
            p = expd[j, :, cols].astype(jnp.float32) * inverse[:, part]
            ds = (p * (scores[j, :, cols] - row_dot[:, part])).astype(jnp.bfloat16)
            pbuf[:, cols] = p.astype(jnp.bfloat16)
            dsbuf[:, cols] = ds
            dq_acc[:, cols] += nn_dot(kt[...], ds)
        dk = nn_dot(dsbuf[...], qs[...])
        dv = nn_dot(pbuf[...], gs[...])

        @pl.when(j < reach)
        def _():
            ret[j, :, 0:HEAD_WIDTH] = dk.astype(jnp.bfloat16)
            ret[j, :, HEAD_WIDTH : 2 * HEAD_WIDTH] = dv.astype(jnp.bfloat16)

        @pl.when(j == reach)
        def _():
            own_acc[:, 0:HEAD_WIDTH] = dk
            own_acc[:, HEAD_WIDTH : 2 * HEAD_WIDTH] = dv

        return 0

    lax.fori_loop(low, reach + 1, grad_step, 0)

    sent = [(own_acc, own_out_ref), (ret.at[reach - jnp.where(odd == 1, 1, reach - 1)], jump_out)]
    for k in range(1, half + 1):
        sent.append((ret.at[reach - 2 * k], z_outs[k]))
        if k < half:
            sent.append((ret.at[reach - (2 * k - 1 + 2 * odd)], y_outs[k]))
    outs = [
        pltpu.make_async_copy(src, dst, out_sems.at[index]) for index, (src, dst) in enumerate(sent)
    ]
    for copy in outs:
        copy.start()
    for g in range(group):
        piece = (dq_acc[:, g * T : (g + 1) * T] * factor).T
        dq_out[:, g * HEAD_WIDTH : (g + 1) * HEAD_WIDTH] = piece.astype(jnp.bfloat16)
    outs.append(pltpu.make_async_copy(dq_out, dq_ref.at[:, g_cols], out_sems.at[reach + 1]))
    outs[-1].start()
    for copy in outs:
        copy.wait()


def head_call(h, reach, group, n_tp, queries, own_grad, grads, kvd, jump, ys, zs, dq):
    T, q_width = queries.shape
    window = reach + 1
    W = group * HEAD_WIDTH
    first = dq is None
    args = [queries, own_grad, *grads, kvd, jump, *ys, *zs] + ([] if first else [dq])
    flops = 5 * 2 * T * (window * T) * W
    bf16, f32 = jnp.bfloat16, jnp.float32
    outs = pl.pallas_call(
        functools.partial(main_kernel, h, reach, group, n_tp, first),
        out_shape=(jax.ShapeDtypeStruct((T, q_width), bf16),)
        + (jax.ShapeDtypeStruct((T, 2 * HEAD_WIDTH), bf16),) * reach
        + (jax.ShapeDtypeStruct((T, 2 * HEAD_WIDTH), f32),),
        in_specs=[ANY] * len(args),
        out_specs=(ANY,) * (reach + 2),
        input_output_aliases={} if first else {len(args) - 1: 0},
        scratch_shapes=[
            pltpu.VMEM((window, T + PAD, 2 * HEAD_WIDTH), bf16),
            pltpu.VMEM((HEAD_WIDTH, T), bf16),
            pltpu.VMEM((group * T, HEAD_WIDTH), bf16),
            pltpu.VMEM((group * T, HEAD_WIDTH), bf16),
            pltpu.VMEM((T, W), bf16),
            pltpu.VMEM((T, W), bf16),
            pltpu.VMEM((window, T, group * T), f32),
            pltpu.VMEM((window, T, group * T), bf16),
            pltpu.VMEM((T, group * T), bf16),
            pltpu.VMEM((T, group * T), bf16),
            pltpu.VMEM((HEAD_WIDTH, group * T), f32),
            pltpu.VMEM((reach, T, 2 * HEAD_WIDTH), bf16),
            pltpu.VMEM((T, 2 * HEAD_WIDTH), f32),
            pltpu.VMEM((8, group * T), f32),
            pltpu.VMEM((8, group * T), f32),
            pltpu.VMEM((8, group * T), f32),
            pltpu.VMEM((T, W), bf16),
            pltpu.SemaphoreType.DMA((reach + 2 + n_tp,)),
            pltpu.SemaphoreType.DMA((reach + 2,)),
        ],
        compiler_params=pltpu.CompilerParams(vmem_limit_bytes=56 * 1024 * 1024),
        cost_estimate=pl.CostEstimate(
            flops=flops, bytes_accessed=4 * 1024 * 1024, transcendentals=T * window * T * group
        ),
    )(*args)
    half = reach // 2
    return outs[0], outs[1], outs[2 : half + 1], outs[half + 1 : -1], outs[-1]


def local(queries, key_matrix, value_matrix, output_gradient, document):
    n = lax.axis_size("seq")
    n_tp = lax.axis_size("tp")
    T, q_width = queries.shape
    heads = key_matrix.shape[1] // HEAD_WIDTH
    group = q_width // (heads * HEAD_WIDTH)
    reach = n // 2
    half = reach // 2

    kvds, chunks = prep(key_matrix, value_matrix, document, output_gradient, n_tp)

    swap = [(a, a ^ 1) for a in range(n)]
    up = [(a, (a + 2) % n) for a in range(n)]
    down = [(b, a) for a, b in up]
    jump = [(a, (a + (reach - 1 if a % 2 else 1)) % n) for a in range(n)]
    jump_back = [(b, a) for a, b in jump]

    def trade(h, m):
        return lax.ppermute(chunks[h][m - 1], "tp", [(a, a ^ m) for a in range(n_tp)])

    arrived = []
    for h in range(heads):
        block = kvds[h]
        if h:
            block = after(block, arrived[-1][2][0])
        zs = [lax.ppermute(block, "seq", up)]
        far = lax.ppermute(block, "seq", jump)
        ys = []
        for k in range(1, half):
            ys.append(lax.ppermute(zs[-1], "seq", swap))
            zs.append(lax.ppermute(zs[-1], "seq", up))
        arrived.append((far, ys, zs))
    grads = [[trade(h, m) for m in range(1, n_tp)] for h in range(heads)]

    def add(*parts):
        return sum(part.astype(jnp.float32) for part in parts)

    factor = 1.0 / math.sqrt(HEAD_WIDTH)
    dq = None
    leaving = []
    for h in range(heads):
        far, ys, zs = arrived[h]
        dq, far, ys, zs, own = head_call(
            h, reach, group, n_tp, queries, output_gradient, grads[h], kvds[h], far, ys, zs, dq
        )
        far = lax.ppermute(far, "seq", jump_back)
        ys = [lax.ppermute(y, "seq", swap) for y in ys]
        leaving.append((far, ys, zs, lax.ppermute(zs[-1], "seq", down), own))
    keys, values = [], []
    for h in range(heads):
        far, ys, zs, moving, own = leaving[h]
        for k in range(half - 1, 0, -1):
            if h < heads - 1:
                moving = after(moving, dq)
            moving = add(moving, zs[k - 1], ys[k - 1]).astype(jnp.bfloat16)
            moving = lax.ppermute(moving, "seq", down)
        total = add(own, far, moving)
        keys.append((total[:, :HEAD_WIDTH] * factor).astype(jnp.bfloat16))
        values.append(total[:, HEAD_WIDTH:].astype(jnp.bfloat16))
    return (dq, jnp.concatenate(keys, axis=1), jnp.concatenate(values, axis=1))


def solution(mesh):
    return jax.shard_map(
        local,
        mesh=mesh,
        in_specs=(P("seq", "tp"), P("seq", "tp"), P("seq", "tp"), P(("seq", "tp"), None), P("seq")),
        out_specs=(P("seq", "tp"), P("seq", "tp"), P("seq", "tp")),
        check_vma=False,
    )
```

```python
import functools
import math

import jax
import jax.numpy as jnp
from jax import lax
from jax.experimental import pallas as pl
from jax.experimental.pallas import tpu as pltpu
from jax.sharding import PartitionSpec as P

HEAD_WIDTH = 128
DOCS = 8
PAD = 16
NEG = -1e30
ANY = pl.BlockSpec(memory_space=pl.ANY)
VMEM = pl.BlockSpec(memory_space=pltpu.VMEM)
SMALL = pltpu.CompilerParams(vmem_limit_bytes=2 * 1024 * 1024)


def prepare_kernel(n_tp, heads, key_ref, value_ref, doc_ref, grad_ref, query_ref, *rest):
    outs, (doc_scr, sems) = rest[:-2], rest[-2:]
    block_out, query_out, own_out, beside_out, across_outs = *outs[:4], outs[4:]
    tokens = key_ref.shape[0]
    rows = grad_ref.shape[0]
    me = lax.axis_index("tp")
    width = grad_ref.shape[1] // n_tp
    copies = []

    def add(src, dst):
        copies.append(pltpu.make_async_copy(src, dst, sems.at[len(copies)]))
        copies[-1].start()

    def columns(m):
        return grad_ref.at[:, pl.ds(pl.multiple_of((me ^ m) * width, width), width)]

    add(doc_ref, doc_scr)
    for h in range(heads):
        for part, src in enumerate((key_ref, value_ref)):
            cols = pl.ds((2 * h + part) * HEAD_WIDTH, HEAD_WIDTH)
            add(
                src.at[:, pl.ds(h * HEAD_WIDTH, HEAD_WIDTH)],
                block_out.at[pl.ds(0, tokens), cols],
            )
    for m in range(2, n_tp):
        add(columns(m), across_outs[m // 2 - 1].at[pl.ds(m % 2 * rows, rows), :])
    add(columns(1), beside_out)
    add(columns(0), own_out)
    add(query_ref, query_out)
    copies[0].wait()
    row = doc_scr[...].astype(jnp.float32).astype(jnp.bfloat16)
    row = jnp.concatenate([row] * heads, axis=1)
    block_out[tokens : tokens + PAD, :] = jnp.broadcast_to(row, (PAD, row.shape[1]))
    for copy in copies[1:]:
        copy.wait()


def prepare(key_matrix, value_matrix, document, output_gradient, queries, n_tp):
    tokens, kv_width = key_matrix.shape
    heads = kv_width // HEAD_WIDTH
    rows, width = output_gradient.shape
    chips = n_tp // 2 - 1
    one = pltpu.VMEM((rows, width // n_tp), jnp.bfloat16)
    two = pltpu.VMEM((2 * rows, width // n_tp), jnp.bfloat16)
    shapes = (
        pltpu.VMEM((tokens + PAD, 2 * kv_width), jnp.bfloat16),
        pltpu.VMEM(queries.shape, jnp.bfloat16),
        one,
        one,
    ) + (two,) * chips
    args = (key_matrix, value_matrix, document.reshape(1, tokens), output_gradient, queries)
    block, query, own, beside, *across = pl.pallas_call(
        functools.partial(prepare_kernel, n_tp, heads),
        out_shape=shapes,
        in_specs=[ANY] * len(args),
        out_specs=(VMEM,) * len(shapes),
        scratch_shapes=[
            pltpu.VMEM((1, tokens), jnp.int32),
            pltpu.SemaphoreType.DMA((2 * heads + n_tp + 2,)),
        ],
        compiler_params=SMALL,
    )(*[pltpu.with_memory_space_constraint(x, pltpu.HBM) for x in args])
    return block, query, own, beside, across


def choose_kernel(even_ref, odd_ref, out_ref):
    odd = lax.rem(lax.axis_index("seq"), 2) == 1

    @pl.when(odd)
    def _():
        out_ref[...] = odd_ref[...]

    @pl.when(jnp.logical_not(odd))
    def _():
        out_ref[...] = even_ref[...]


def choose(even, odd):
    return pl.pallas_call(
        choose_kernel,
        out_shape=pltpu.VMEM(even.shape, even.dtype),
        in_specs=[VMEM, VMEM],
        out_specs=VMEM,
        compiler_params=SMALL,
    )(*held(even, odd))


def lower_kernel(pair_ref, out_ref):
    out_ref[...] = pair_ref[out_ref.shape[0] :, :]


def lower(pair):
    rows, width = pair.shape
    return pl.pallas_call(
        lower_kernel,
        out_shape=pltpu.VMEM((rows // 2, width), pair.dtype),
        in_specs=[VMEM],
        out_specs=VMEM,
        compiler_params=SMALL,
    )(*held(pair))


def relay_kernel(near, *refs):
    total = refs[0][...].astype(jnp.float32)
    for ref in refs[1 : -2 if near else -1]:
        total = total + ref[...].astype(jnp.float32)
    if near:
        odd = lax.rem(lax.axis_index("seq"), 2) == 1
        total = total + jnp.where(odd, refs[-2][...].astype(jnp.float32), 0.0)
    refs[-1][...] = total.astype(refs[-1].dtype)


def relay(near, *parts):
    return pl.pallas_call(
        functools.partial(relay_kernel, near),
        out_shape=pltpu.VMEM(parts[0].shape, jnp.bfloat16),
        in_specs=[VMEM] * len(parts),
        out_specs=VMEM,
        compiler_params=SMALL,
    )(*held(*parts))


def finish_kernel(heads, *refs):
    key_out, value_out = refs[-2:]
    even = lax.rem(lax.axis_index("seq"), 2) == 0
    factor = 1.0 / math.sqrt(HEAD_WIDTH)
    for h in range(heads):
        own, moved, near = refs[3 * h : 3 * h + 3]
        total = own[...] + moved[...].astype(jnp.float32)
        total = total + jnp.where(even, near[...].astype(jnp.float32), 0.0)
        cols = slice(h * HEAD_WIDTH, (h + 1) * HEAD_WIDTH)
        key_out[:, cols] = (total[:, :HEAD_WIDTH] * factor).astype(jnp.bfloat16)
        value_out[:, cols] = total[:, HEAD_WIDTH:].astype(jnp.bfloat16)


def finish(*parts):
    heads = len(parts) // 3
    out = jax.ShapeDtypeStruct((parts[0].shape[0], heads * HEAD_WIDTH), jnp.bfloat16)
    return pl.pallas_call(
        functools.partial(finish_kernel, heads),
        out_shape=(out, out),
        in_specs=[VMEM] * len(parts),
        out_specs=(VMEM, VMEM),
        compiler_params=SMALL,
    )(*held(*parts))


def held(*arrays):
    return [pltpu.with_memory_space_constraint(x, pltpu.VMEM) for x in arrays]


def after(array, *others):
    return lax.optimization_barrier((array, *others))[0]


def nt_dot(a, b):
    return lax.dot_general(a, b, (((1,), (1,)), ((), ())), preferred_element_type=jnp.float32)


def nn_dot(a, b):
    return lax.dot_general(a, b, (((1,), (0,)), ((), ())), preferred_element_type=jnp.float32)


def main_kernel(h, reach, group, n_tp, first, *refs):
    half = reach // 2
    refs = list(refs)
    take = lambda count: [refs.pop(0) for _ in range(count)]
    (query_ref,) = take(1)
    grad_refs = take(n_tp)
    (own_ref,) = take(1)
    odd_refs = take(half)
    even_refs = take(half)
    if not first:
        take(1)
    (dq_ref,) = take(1)
    odd_outs = take(half)
    even_outs = take(half)
    (own_out_ref,) = take(1)
    (kx, vx, kt, qx, gs) = take(5)
    scores, peaks, grads, weights, stats = take(2), take(2), take(2), take(2), take(2)
    (dk_acc, dv_acc, dq_out, out_sems) = take(4)

    T = own_out_ref.shape[0]
    W = group * HEAD_WIDTH
    i = lax.axis_index("seq")
    t = lax.axis_index("tp")
    sub = T // n_tp
    window = (reach + 1) * T
    block_refs = [own_ref]
    for k in range(half):
        block_refs += [odd_refs[k], even_refs[k]]
    dk_acc[...] = jnp.zeros(dk_acc.shape, jnp.float32)
    dv_acc[...] = jnp.zeros(dv_acc.shape, jnp.float32)

    code = lax.broadcasted_iota(jnp.int32, (HEAD_WIDTH, T), 0).astype(jnp.float32)
    at = 2 * h * HEAD_WIDTH
    for d, block in enumerate(block_refs):
        row = block[T : T + 1, at : at + T].astype(jnp.float32)
        row = jnp.where(i >= d, row, float(DOCS))
        one_hot = jnp.where(code == row, 1.0, 0.0).astype(jnp.bfloat16)
        kx[reach - d, :, 0:HEAD_WIDTH] = block[0:T, at : at + HEAD_WIDTH]
        kx[reach - d, :, HEAD_WIDTH : 2 * HEAD_WIDTH] = one_hot.T
        vx[reach - d] = block[0:T, at + HEAD_WIDTH : at + 2 * HEAD_WIDTH]
    own_row = own_ref[T : T + 1, at : at + T].astype(jnp.float32)
    away = jnp.where((code == own_row) | (code > DOCS), 0.0, NEG).astype(jnp.bfloat16).T
    for g in range(group):
        at = (h * group + g) * HEAD_WIDTH
        qx[g, :, 0:HEAD_WIDTH] = query_ref[:, at : at + HEAD_WIDTH]
        qx[g, :, HEAD_WIDTH : 2 * HEAD_WIDTH] = away

    factor = 1.0 / math.sqrt(HEAD_WIDTH)
    scale = factor * math.log2(math.e)
    before = reach * T

    def by_eight(x):
        return x.reshape(x.shape[0] // 8, 8, T)

    def dq_copy(g):
        cols = pl.ds(pl.multiple_of((h * group + g) * HEAD_WIDTH, HEAD_WIDTH), HEAD_WIDTH)
        return pltpu.make_async_copy(dq_out.at[g], dq_ref.at[:, cols], out_sems.at[g])

    def step(score_of, weight_of, grad_of, b):
        c = 1 - b
        if score_of is not None:
            s = nt_dot(kx[...].reshape(window, 2 * HEAD_WIDTH), qx[score_of])
            causal = lax.broadcasted_iota(jnp.int32, (T, T), 0) <= lax.broadcasted_iota(
                jnp.int32, (T, T), 1
            )
            own = jnp.where(causal, s[before:], NEG)
            scores[b][0:before] = s[:before]
            scores[b][before:] = own
            peaks[b][...] = jnp.maximum(
                jnp.max(by_eight(s[:before]), axis=0), jnp.max(by_eight(own), axis=0)
            )
        if weight_of is not None:
            top = jnp.max(peaks[c][...], axis=0, keepdims=True) * scale
            dp = nt_dot(vx[...].reshape(window, HEAD_WIDTH), gs[weight_of])
            e = jnp.exp2(scores[c][...] * scale - top)
            weights[c][...] = e.astype(jnp.bfloat16)
            grads[c][...] = dp
            total = jnp.sum(jnp.sum(by_eight(e), axis=0), axis=0, keepdims=True)
            weighted = jnp.sum(jnp.sum(by_eight(e * dp), axis=0), axis=0, keepdims=True)
            stats[c][0:1] = 1.0 / total
            stats[c][1:2] = weighted / total
        if grad_of is not None:
            inverse = stats[b][0:1]
            e_old = weights[b][...]
            ds = (e_old.astype(jnp.float32) * (grads[b][...] - stats[b][1:2])).astype(jnp.bfloat16)
            column = jnp.broadcast_to(inverse, (HEAD_WIDTH, T)).T
            query = (qx[grad_of, :, 0:HEAD_WIDTH].astype(jnp.float32) * column).astype(jnp.bfloat16)
            grad = (gs[grad_of].astype(jnp.float32) * column).astype(jnp.bfloat16)
        if grad_of is not None:
            dq = nn_dot(kt[...], ds) * (inverse * factor)
            dq_out[grad_of] = dq.T.astype(jnp.bfloat16)
            dq_copy(grad_of).start()
            dv_acc[...] += nn_dot(e_old, grad)
            dk_acc[...] += nn_dot(ds, query)

    def two_steps(pair, _):
        g = 2 * pair
        step(g + 2, g + 1, g, 0)
        step(g + 3, g + 2, g + 1, 1)
        return 0

    step(0, None, None, 0)
    for d in range(reach + 1):
        kt[:, (reach - d) * T : (reach - d + 1) * T] = kx[reach - d, :, 0:HEAD_WIDTH].T
    for m in range(n_tp):
        rows = pl.ds(pl.multiple_of((t ^ m) * sub, sub), sub)
        src = grad_refs[m]
        for g in range(group):
            at = h * W + g * HEAD_WIDTH
            gs[g, rows, :] = src[0:sub, at : at + HEAD_WIDTH]
    step(1, 0, None, 1)
    lax.fori_loop(0, group // 2 - 1, two_steps, 0)
    step(None, group - 1, group - 2, 0)
    step(None, None, group - 1, 1)

    for d in range(reach + 1):
        dst = (odd_outs if d % 2 else even_outs)[(d - 1) // 2] if d else own_out_ref
        rows = slice((reach - d) * T, (reach - d + 1) * T)
        dst[:, 0:HEAD_WIDTH] = dk_acc[rows, :].astype(dst.dtype)
        dst[:, HEAD_WIDTH : 2 * HEAD_WIDTH] = dv_acc[rows, :].astype(dst.dtype)
    for g in range(group):
        dq_copy(g).wait()


def scratch_of(window, T, group):
    bf16, f32 = jnp.bfloat16, jnp.float32
    return [
        pltpu.VMEM((window, T, 2 * HEAD_WIDTH), bf16),
        pltpu.VMEM((window, T, HEAD_WIDTH), bf16),
        pltpu.VMEM((HEAD_WIDTH, window * T), bf16),
        pltpu.VMEM((group, T, 2 * HEAD_WIDTH), bf16),
        pltpu.VMEM((group, T, HEAD_WIDTH), bf16),
        *[pltpu.VMEM((window * T, T), f32)] * 2,
        *[pltpu.VMEM((8, T), f32)] * 2,
        *[pltpu.VMEM((window * T, T), f32)] * 2,
        *[pltpu.VMEM((window * T, T), bf16)] * 2,
        *[pltpu.VMEM((8, T), f32)] * 2,
        pltpu.VMEM((window * T, HEAD_WIDTH), f32),
        pltpu.VMEM((window * T, HEAD_WIDTH), f32),
        pltpu.VMEM((group, T, HEAD_WIDTH), bf16),
    ]


def head_call(h, reach, group, n_tp, queries, grads, block, odds, evens, dq):
    T, q_width = queries.shape
    window = reach + 1
    first = dq is None
    args = held(queries, *grads, block, *odds, *evens)
    specs = [VMEM] * len(args)
    if not first:
        args.append(dq)
        specs.append(ANY)
    flops = 5 * 2 * T * (window * T) * group * HEAD_WIDTH
    scratch = scratch_of(window, T, group)
    outs = pl.pallas_call(
        functools.partial(main_kernel, h, reach, group, n_tp, first),
        out_shape=(pltpu.HBM((T, q_width), jnp.bfloat16),)
        + (pltpu.VMEM((T, 2 * HEAD_WIDTH), jnp.bfloat16),) * reach
        + (pltpu.VMEM((T, 2 * HEAD_WIDTH), jnp.float32),),
        in_specs=specs,
        out_specs=(ANY,) + (VMEM,) * (reach + 1),
        input_output_aliases={} if first else {len(args) - 1: 0},
        scratch_shapes=[*scratch, pltpu.SemaphoreType.DMA((group,))],
        compiler_params=pltpu.CompilerParams(
            vmem_limit_bytes=2 * sum(math.prod(x.shape) * x.dtype.itemsize for x in scratch)
        ),
        cost_estimate=pl.CostEstimate(
            flops=4 * flops,
            bytes_accessed=4 * 1024 * 1024,
            transcendentals=T * window * T * group,
        ),
    )(*args)
    half = reach // 2
    return outs[0], outs[1 : half + 1], outs[half + 1 : -1], outs[-1]


def local(queries, key_matrix, value_matrix, output_gradient, document):
    n = lax.axis_size("seq")
    n_tp = lax.axis_size("tp")
    T, q_width = queries.shape
    heads = key_matrix.shape[1] // HEAD_WIDTH
    group = q_width // (heads * HEAD_WIDTH)
    reach = n // 2
    half = reach // 2

    block, queries, mine, beside, across = prepare(
        key_matrix, value_matrix, document, output_gradient, queries, n_tp
    )

    swap = [(a, a ^ 1) for a in range(n)]
    one_up = [(a, (a + 1) % n) for a in range(n)]
    two_up = [(a, (a + 2) % n) for a in range(n)]
    one_down = [(b, a) for a, b in one_up]
    two_down = [(b, a) for a, b in two_up]
    cores = [(a, a ^ 1) for a in range(n_tp)]

    evens = [lax.ppermute(block, "seq", two_up)]
    pairs = [
        lax.ppermute(pair, "tp", [(a, a ^ (2 * m + 2)) for a in range(n_tp)])
        for m, pair in enumerate(across)
    ]
    odds = [None]
    for k in range(1, half):
        odds.append(lax.ppermute(evens[-1], "seq", one_up))
        evens.append(lax.ppermute(evens[-1], "seq", two_up))
    odds[0] = lax.ppermute(choose(block, evens[0]), "seq", swap)
    grads = [mine, lax.ppermute(beside, "tp", cores)]
    for pair in pairs:
        grads += [pair, lax.ppermute(lower(pair), "tp", cores)]

    dq = None
    odds_in, evens_in = odds, evens
    leaving = []
    for h in range(heads):
        dq, odds, evens, own = head_call(
            h, reach, group, n_tp, queries, grads, block, odds_in, evens_in, dq
        )
        last = evens[-1]
        if leaving:
            moved = [*leaving[-1][0], leaving[-1][2]]
            odds = [after(x, *moved) for x in odds]
            last = after(last, *moved)
        moving = lax.ppermute(last, "seq", two_down)
        odds = [lax.ppermute(x, "seq", one_down if k else swap) for k, x in enumerate(odds)]
        leaving.append((odds, evens, moving, own))
    ends = []
    for h in range(heads):
        odds, evens, moving, own = leaving[h]
        for k in range(half - 1, 0, -1):
            if h < heads - 1:
                moving = after(moving, dq)
            parts = [moving, evens[k - 1], odds[k]] + ([odds[0]] if k == 1 else [])
            moving = lax.ppermute(relay(k == 1, *parts), "seq", two_down)
        ends += [own, moving, odds[0]]
    return (dq, *finish(*ends))


def solution(mesh):
    return jax.shard_map(
        local,
        mesh=mesh,
        in_specs=(P("seq", "tp"), P("seq", "tp"), P("seq", "tp"), P(("seq", "tp"), None), P("seq")),
        out_specs=(P("seq", "tp"), P("seq", "tp"), P("seq", "tp")),
        check_vma=False,
    )
```

```python
import functools
import math

import jax
import jax.numpy as jnp
from jax import lax
from jax.experimental import pallas as pl
from jax.experimental.pallas import tpu as pltpu
from jax.sharding import PartitionSpec as P

HEAD_WIDTH = 128
DOCS = 8
PAD = 16
NEG = -1e30
ANY = pl.BlockSpec(memory_space=pl.ANY)
VMEM = pl.BlockSpec(memory_space=pltpu.VMEM)
SMALL = pltpu.CompilerParams(vmem_limit_bytes=2 * 1024 * 1024)


def prepare_kernel(n_tp, heads, key_ref, value_ref, doc_ref, grad_ref, query_ref, *rest):
    outs, (doc_scr, sems) = rest[:-2], rest[-2:]
    block_out, query_out, own_out, beside_out, across_outs = *outs[:4], outs[4:]
    tokens = key_ref.shape[0]
    rows = grad_ref.shape[0]
    me = lax.axis_index("tp")
    width = grad_ref.shape[1] // n_tp
    copies = []

    def add(src, dst):
        copies.append(pltpu.make_async_copy(src, dst, sems.at[len(copies)]))
        copies[-1].start()

    def columns(m):
        return grad_ref.at[:, pl.ds(pl.multiple_of((me ^ m) * width, width), width)]

    add(doc_ref, doc_scr)
    for h in range(heads):
        for part, src in enumerate((key_ref, value_ref)):
            cols = pl.ds((2 * h + part) * HEAD_WIDTH, HEAD_WIDTH)
            add(
                src.at[:, pl.ds(h * HEAD_WIDTH, HEAD_WIDTH)],
                block_out.at[pl.ds(0, tokens), cols],
            )
    for m in range(2, n_tp):
        add(columns(m), across_outs[m // 2 - 1].at[pl.ds(m % 2 * rows, rows), :])
    add(columns(1), beside_out)
    add(columns(0), own_out)
    add(query_ref, query_out)
    copies[0].wait()
    row = doc_scr[...].astype(jnp.float32).astype(jnp.bfloat16)
    row = jnp.concatenate([row] * heads, axis=1)
    block_out[tokens : tokens + PAD, :] = jnp.broadcast_to(row, (PAD, row.shape[1]))
    for copy in copies[1:]:
        copy.wait()


def prepare(key_matrix, value_matrix, document, output_gradient, queries, n_tp):
    tokens, kv_width = key_matrix.shape
    heads = kv_width // HEAD_WIDTH
    rows, width = output_gradient.shape
    chips = n_tp // 2 - 1
    one = pltpu.VMEM((rows, width // n_tp), jnp.bfloat16)
    two = pltpu.VMEM((2 * rows, width // n_tp), jnp.bfloat16)
    shapes = (
        pltpu.VMEM((tokens + PAD, 2 * kv_width), jnp.bfloat16),
        pltpu.VMEM(queries.shape, jnp.bfloat16),
        one,
        one,
    ) + (two,) * chips
    args = (key_matrix, value_matrix, document.reshape(1, tokens), output_gradient, queries)
    block, query, own, beside, *across = pl.pallas_call(
        functools.partial(prepare_kernel, n_tp, heads),
        out_shape=shapes,
        in_specs=[ANY] * len(args),
        out_specs=(VMEM,) * len(shapes),
        scratch_shapes=[
            pltpu.VMEM((1, tokens), jnp.int32),
            pltpu.SemaphoreType.DMA((2 * heads + n_tp + 2,)),
        ],
        compiler_params=SMALL,
    )(*[pltpu.with_memory_space_constraint(x, pltpu.HBM) for x in args])
    return block, query, own, beside, across


def choose_kernel(even_ref, odd_ref, out_ref):
    odd = lax.rem(lax.axis_index("seq"), 2) == 1

    @pl.when(odd)
    def _():
        out_ref[...] = odd_ref[...]

    @pl.when(jnp.logical_not(odd))
    def _():
        out_ref[...] = even_ref[...]


def choose(even, odd):
    return pl.pallas_call(
        choose_kernel,
        out_shape=pltpu.VMEM(even.shape, even.dtype),
        in_specs=[VMEM, VMEM],
        out_specs=VMEM,
        compiler_params=SMALL,
    )(*held(even, odd))


def lower_kernel(pair_ref, out_ref):
    out_ref[...] = pair_ref[out_ref.shape[0] :, :]


def lower(pair):
    rows, width = pair.shape
    return pl.pallas_call(
        lower_kernel,
        out_shape=pltpu.VMEM((rows // 2, width), pair.dtype),
        in_specs=[VMEM],
        out_specs=VMEM,
        compiler_params=SMALL,
    )(*held(pair))


def relay_kernel(near, *refs):
    total = refs[0][...].astype(jnp.float32)
    for ref in refs[1 : -2 if near else -1]:
        total = total + ref[...].astype(jnp.float32)
    if near:
        odd = lax.rem(lax.axis_index("seq"), 2) == 1
        total = total + jnp.where(odd, refs[-2][...].astype(jnp.float32), 0.0)
    refs[-1][...] = total.astype(refs[-1].dtype)


def relay(near, *parts):
    return pl.pallas_call(
        functools.partial(relay_kernel, near),
        out_shape=pltpu.VMEM(parts[0].shape, jnp.bfloat16),
        in_specs=[VMEM] * len(parts),
        out_specs=VMEM,
        compiler_params=SMALL,
    )(*held(*parts))


def finish_kernel(heads, *refs):
    key_out, value_out = refs[-2:]
    even = lax.rem(lax.axis_index("seq"), 2) == 0
    factor = 1.0 / math.sqrt(HEAD_WIDTH)
    for h in range(heads):
        own, moved, near = refs[3 * h : 3 * h + 3]
        total = own[...] + moved[...].astype(jnp.float32)
        total = total + jnp.where(even, near[...].astype(jnp.float32), 0.0)
        cols = slice(h * HEAD_WIDTH, (h + 1) * HEAD_WIDTH)
        key_out[:, cols] = (total[:, :HEAD_WIDTH] * factor).astype(jnp.bfloat16)
        value_out[:, cols] = total[:, HEAD_WIDTH:].astype(jnp.bfloat16)


def finish(*parts):
    heads = len(parts) // 3
    out = jax.ShapeDtypeStruct((parts[0].shape[0], heads * HEAD_WIDTH), jnp.bfloat16)
    return pl.pallas_call(
        functools.partial(finish_kernel, heads),
        out_shape=(out, out),
        in_specs=[VMEM] * len(parts),
        out_specs=(VMEM, VMEM),
        compiler_params=SMALL,
    )(*held(*parts))


def held(*arrays):
    return [pltpu.with_memory_space_constraint(x, pltpu.VMEM) for x in arrays]


def after(array, *others):
    return lax.optimization_barrier((array, *others))[0]


def nt_dot(a, b):
    return lax.dot_general(a, b, (((1,), (1,)), ((), ())), preferred_element_type=jnp.float32)


def nn_dot(a, b):
    return lax.dot_general(a, b, (((1,), (0,)), ((), ())), preferred_element_type=jnp.float32)


def main_kernel(h, reach, group, n_tp, first, *refs):
    half = reach // 2
    refs = list(refs)
    take = lambda count: [refs.pop(0) for _ in range(count)]
    (query_ref,) = take(1)
    grad_refs = take(n_tp)
    (own_ref,) = take(1)
    odd_refs = take(half)
    even_refs = take(half)
    if not first:
        take(1)
    (dq_ref,) = take(1)
    odd_outs = take(half)
    even_outs = take(half)
    (own_out_ref,) = take(1)
    (kx, vx, kt, qx, gs) = take(5)
    scores, peaks, grads, weights, stats = take(2), take(2), take(2), take(2), take(2)
    (dk_acc, dv_acc, dq_out, out_sems) = take(4)

    T = own_out_ref.shape[0]
    W = group * HEAD_WIDTH
    i = lax.axis_index("seq")
    t = lax.axis_index("tp")
    sub = T // n_tp
    window = (reach + 1) * T
    block_refs = [own_ref]
    for k in range(half):
        block_refs += [odd_refs[k], even_refs[k]]
    dk_acc[...] = jnp.zeros(dk_acc.shape, jnp.float32)
    dv_acc[...] = jnp.zeros(dv_acc.shape, jnp.float32)

    code = lax.broadcasted_iota(jnp.int32, (HEAD_WIDTH, T), 0).astype(jnp.float32)
    at = 2 * h * HEAD_WIDTH
    for d, block in enumerate(block_refs):
        row = block[T : T + 1, at : at + T].astype(jnp.float32)
        row = jnp.where(i >= d, row, float(DOCS))
        one_hot = jnp.where(code == row, 1.0, 0.0).astype(jnp.bfloat16)
        rows = slice((reach - d) * T, (reach - d + 1) * T)
        kx[rows, 0:HEAD_WIDTH] = block[0:T, at : at + HEAD_WIDTH]
        kx[rows, HEAD_WIDTH : 2 * HEAD_WIDTH] = one_hot.T
        vx[rows, :] = block[0:T, at + HEAD_WIDTH : at + 2 * HEAD_WIDTH]
    own_row = own_ref[T : T + 1, at : at + T].astype(jnp.float32)
    away = jnp.where((code == own_row) | (code > DOCS), 0.0, NEG).astype(jnp.bfloat16).T
    half_rows = T // 2
    for unit in range(group):
        queries_at = slice(unit % 2 * half_rows, (unit % 2 + 1) * half_rows)
        for two in range(2):
            at = (h * group + unit - unit % 2 + two) * HEAD_WIDTH
            rows = slice(two * half_rows, (two + 1) * half_rows)
            qx[unit, rows, 0:HEAD_WIDTH] = query_ref[queries_at, at : at + HEAD_WIDTH]
            qx[unit, rows, HEAD_WIDTH : 2 * HEAD_WIDTH] = away[queries_at, :]

    factor = 1.0 / math.sqrt(HEAD_WIDTH)
    scale = factor * math.log2(math.e)
    seen_rows = window - half_rows
    before = seen_rows - half_rows

    def by_eight(x):
        return x.reshape(x.shape[0] // 8, 8, T)

    def dq_copies(unit, part):
        copies = []
        for two in range(2):
            at = pl.multiple_of((h * group + unit - part + two) * HEAD_WIDTH, HEAD_WIDTH)
            copies.append(
                pltpu.make_async_copy(
                    dq_out.at[unit, pl.ds(two * half_rows, half_rows), :],
                    dq_ref.at[pl.ds(part * half_rows, half_rows), pl.ds(at, HEAD_WIDTH)],
                    out_sems.at[unit, two],
                )
            )
        return copies

    def step(score_of, weight_of, grad_of, b):
        c = 1 - b
        rows = [slice(half_rows * part, half_rows * part + seen_rows) for part in range(2)]
        if score_of is not None:
            s = nt_dot(kx[rows[b], :], qx[score_of])
            query = lax.broadcasted_iota(jnp.int32, (half_rows, T), 1)
            query = jnp.where(query >= half_rows, query - half_rows, query)
            causal = lax.broadcasted_iota(jnp.int32, (half_rows, T), 0) <= query
            own = jnp.where(causal, s[before:], NEG)
            scores[b][0:before] = s[:before]
            scores[b][before:] = own
            peaks[b][...] = jnp.maximum(
                jnp.max(by_eight(s[:before]), axis=0), jnp.max(by_eight(own), axis=0)
            )
        if weight_of is not None:
            top = jnp.max(peaks[c][...], axis=0, keepdims=True) * scale
            dp = nt_dot(vx[rows[c], :], gs[weight_of])
            e = jnp.exp2(scores[c][...] * scale - top)
            weights[c][...] = e.astype(jnp.bfloat16)
            grads[c][...] = dp
            total = jnp.sum(jnp.sum(by_eight(e), axis=0), axis=0, keepdims=True)
            weighted = jnp.sum(jnp.sum(by_eight(e * dp), axis=0), axis=0, keepdims=True)
            stats[c][0:1] = 1.0 / total
            stats[c][1:2] = weighted / total
        if grad_of is not None:
            inverse = stats[b][0:1]
            e_old = weights[b][...]
            ds = (e_old.astype(jnp.float32) * (grads[b][...] - stats[b][1:2])).astype(jnp.bfloat16)
            column = jnp.broadcast_to(inverse, (HEAD_WIDTH, T)).T
            query = (qx[grad_of, :, 0:HEAD_WIDTH].astype(jnp.float32) * column).astype(jnp.bfloat16)
            grad = (gs[grad_of].astype(jnp.float32) * column).astype(jnp.bfloat16)
            dq = nn_dot(kt[:, rows[b]], ds) * (inverse * factor)
            dq_out[grad_of] = dq.T.astype(jnp.bfloat16)
            for copy in dq_copies(grad_of, b):
                copy.start()
            dv_acc[rows[b], :] += nn_dot(e_old, grad)
            dk_acc[rows[b], :] += nn_dot(ds, query)

    def two_steps(pair, _):
        g = 2 * pair
        step(g + 2, g + 1, g, 0)
        step(g + 3, g + 2, g + 1, 1)
        return 0

    step(0, None, None, 0)
    for j in range(reach + 1):
        kt[:, j * T : (j + 1) * T] = kx[j * T : (j + 1) * T, 0:HEAD_WIDTH].T
    for m in range(n_tp):
        first_row = (t ^ m) * sub
        part = first_row // half_rows
        at_row = pl.multiple_of(first_row - part * half_rows, sub)
        for g in range(group):
            at = h * W + g * HEAD_WIDTH
            rows = pl.ds(pl.multiple_of(g % 2 * half_rows + at_row, sub), sub)
            gs[g - g % 2 + part, rows, :] = grad_refs[m][0:sub, at : at + HEAD_WIDTH]
    step(1, 0, None, 1)
    lax.fori_loop(0, group // 2 - 1, two_steps, 0)
    step(None, group - 1, group - 2, 0)
    step(None, None, group - 1, 1)

    for d in range(reach + 1):
        dst = (odd_outs if d % 2 else even_outs)[(d - 1) // 2] if d else own_out_ref
        rows = slice((reach - d) * T, (reach - d + 1) * T)
        dst[:, 0:HEAD_WIDTH] = dk_acc[rows, :].astype(dst.dtype)
        dst[:, HEAD_WIDTH : 2 * HEAD_WIDTH] = dv_acc[rows, :].astype(dst.dtype)
    for unit in range(group):
        for copy in dq_copies(unit, unit % 2):
            copy.wait()


def scratch_of(window, T, group):
    bf16, f32 = jnp.bfloat16, jnp.float32
    return [
        pltpu.VMEM((window * T, 2 * HEAD_WIDTH), bf16),
        pltpu.VMEM((window * T, HEAD_WIDTH), bf16),
        pltpu.VMEM((HEAD_WIDTH, window * T), bf16),
        pltpu.VMEM((group, T, 2 * HEAD_WIDTH), bf16),
        pltpu.VMEM((group, T, HEAD_WIDTH), bf16),
        *[pltpu.VMEM((window * T - T // 2, T), f32)] * 2,
        *[pltpu.VMEM((8, T), f32)] * 2,
        *[pltpu.VMEM((window * T - T // 2, T), f32)] * 2,
        *[pltpu.VMEM((window * T - T // 2, T), bf16)] * 2,
        *[pltpu.VMEM((8, T), f32)] * 2,
        pltpu.VMEM((window * T, HEAD_WIDTH), f32),
        pltpu.VMEM((window * T, HEAD_WIDTH), f32),
        pltpu.VMEM((group, T, HEAD_WIDTH), bf16),
    ]


def head_call(h, reach, group, n_tp, queries, grads, block, odds, evens, dq):
    T, q_width = queries.shape
    window = reach + 1
    first = dq is None
    args = held(queries, *grads, block, *odds, *evens)
    specs = [VMEM] * len(args)
    if not first:
        args.append(dq)
        specs.append(ANY)
    flops = 5 * 2 * T * (window * T) * group * HEAD_WIDTH
    scratch = scratch_of(window, T, group)
    outs = pl.pallas_call(
        functools.partial(main_kernel, h, reach, group, n_tp, first),
        out_shape=(pltpu.HBM((T, q_width), jnp.bfloat16),)
        + (pltpu.VMEM((T, 2 * HEAD_WIDTH), jnp.bfloat16),) * reach
        + (pltpu.VMEM((T, 2 * HEAD_WIDTH), jnp.float32),),
        in_specs=specs,
        out_specs=(ANY,) + (VMEM,) * (reach + 1),
        input_output_aliases={} if first else {len(args) - 1: 0},
        scratch_shapes=[*scratch, pltpu.SemaphoreType.DMA((group, 2))],
        compiler_params=pltpu.CompilerParams(
            vmem_limit_bytes=2 * sum(math.prod(x.shape) * x.dtype.itemsize for x in scratch)
        ),
        cost_estimate=pl.CostEstimate(
            flops=4 * flops,
            bytes_accessed=4 * 1024 * 1024,
            transcendentals=T * window * T * group,
        ),
    )(*args)
    half = reach // 2
    return outs[0], outs[1 : half + 1], outs[half + 1 : -1], outs[-1]


def local(queries, key_matrix, value_matrix, output_gradient, document):
    n = lax.axis_size("seq")
    n_tp = lax.axis_size("tp")
    T, q_width = queries.shape
    heads = key_matrix.shape[1] // HEAD_WIDTH
    group = q_width // (heads * HEAD_WIDTH)
    reach = n // 2
    half = reach // 2

    block, queries, mine, beside, across = prepare(
        key_matrix, value_matrix, document, output_gradient, queries, n_tp
    )

    swap = [(a, a ^ 1) for a in range(n)]
    one_up = [(a, (a + 1) % n) for a in range(n)]
    two_up = [(a, (a + 2) % n) for a in range(n)]
    one_down = [(b, a) for a, b in one_up]
    two_down = [(b, a) for a, b in two_up]
    cores = [(a, a ^ 1) for a in range(n_tp)]

    evens = [lax.ppermute(block, "seq", two_up)]
    pairs = [
        lax.ppermute(pair, "tp", [(a, a ^ (2 * m + 2)) for a in range(n_tp)])
        for m, pair in enumerate(across)
    ]
    odds = [None]
    for k in range(1, half):
        odds.append(lax.ppermute(evens[-1], "seq", one_up))
        evens.append(lax.ppermute(evens[-1], "seq", two_up))
    odds[0] = lax.ppermute(choose(block, evens[0]), "seq", swap)
    grads = [mine, lax.ppermute(beside, "tp", cores)]
    for pair in pairs:
        grads += [pair, lax.ppermute(lower(pair), "tp", cores)]

    dq = None
    odds_in, evens_in = odds, evens
    leaving = []
    for h in range(heads):
        dq, odds, evens, own = head_call(
            h, reach, group, n_tp, queries, grads, block, odds_in, evens_in, dq
        )
        last = evens[-1]
        if leaving:
            moved = [*leaving[-1][0], leaving[-1][2]]
            odds = [after(x, *moved) for x in odds]
            last = after(last, *moved)
        moving = lax.ppermute(last, "seq", two_down)
        odds = [lax.ppermute(x, "seq", one_down if k else swap) for k, x in enumerate(odds)]
        leaving.append((odds, evens, moving, own))
    ends = []
    for h in range(heads):
        odds, evens, moving, own = leaving[h]
        for k in range(half - 1, 0, -1):
            if h < heads - 1:
                moving = after(moving, dq)
            parts = [moving, evens[k - 1], odds[k]] + ([odds[0]] if k == 1 else [])
            moving = lax.ppermute(relay(k == 1, *parts), "seq", two_down)
        ends += [own, moving, odds[0]]
    return (dq, *finish(*ends))


def solution(mesh):
    return jax.shard_map(
        local,
        mesh=mesh,
        in_specs=(P("seq", "tp"), P("seq", "tp"), P("seq", "tp"), P(("seq", "tp"), None), P("seq")),
        out_specs=(P("seq", "tp"), P("seq", "tp"), P("seq", "tp")),
        check_vma=False,
    )
```

```python
import functools
import math

import jax
import jax.numpy as jnp
from jax import lax
from jax.experimental import pallas as pl
from jax.experimental.pallas import tpu as pltpu
from jax.sharding import PartitionSpec as P

HEAD_WIDTH = 128
DOCS = 8
PAD = 16
NEG = -1e30
ANY = pl.BlockSpec(memory_space=pl.ANY)
VMEM = pl.BlockSpec(memory_space=pltpu.VMEM)
SMALL = pltpu.CompilerParams(vmem_limit_bytes=2 * 1024 * 1024)


def prepare_kernel(n_tp, heads, key_ref, value_ref, doc_ref, grad_ref, query_ref, *rest):
    outs, (doc_scr, sems) = rest[:-2], rest[-2:]
    block_out, query_out, own_out, beside_out, across_outs = *outs[:4], outs[4:]
    tokens = key_ref.shape[0]
    rows = grad_ref.shape[0]
    me = lax.axis_index("tp")
    width = grad_ref.shape[1] // n_tp
    copies = []

    def add(src, dst):
        copies.append(pltpu.make_async_copy(src, dst, sems.at[len(copies)]))
        copies[-1].start()

    def columns(m, at, size):
        start = pl.multiple_of((me ^ m) * width + at, size)
        return grad_ref.at[:, pl.ds(start, size)]

    add(doc_ref, doc_scr)
    for h in range(heads):
        for part, src in enumerate((key_ref, value_ref)):
            cols = pl.ds((2 * h + part) * HEAD_WIDTH, HEAD_WIDTH)
            add(
                src.at[:, pl.ds(h * HEAD_WIDTH, HEAD_WIDTH)],
                block_out.at[pl.ds(0, tokens), cols],
            )
    part = width // heads
    for m in range(2, n_tp):
        for h in range(heads):
            out = across_outs[(m // 2 - 1) * heads + h]
            src = columns(m, h * part, part)
            add(src, out.at[pl.ds(m % 2 * rows, rows), :])
    add(columns(1, 0, width), beside_out)
    add(columns(0, 0, width), own_out)
    add(query_ref, query_out)
    copies[0].wait()
    row = doc_scr[...].astype(jnp.float32).astype(jnp.bfloat16)
    row = jnp.concatenate([row] * heads, axis=1)
    block_out[tokens : tokens + PAD, :] = jnp.broadcast_to(row, (PAD, row.shape[1]))
    for copy in copies[1:]:
        copy.wait()


def prepare(key_matrix, value_matrix, document, output_gradient, queries, n_tp):
    tokens, kv_width = key_matrix.shape
    heads = kv_width // HEAD_WIDTH
    rows, width = output_gradient.shape
    chips = n_tp // 2 - 1
    one = pltpu.VMEM((rows, width // n_tp), jnp.bfloat16)
    two = pltpu.VMEM((2 * rows, width // n_tp // heads), jnp.bfloat16)
    shapes = (
        pltpu.VMEM((tokens + PAD, 2 * kv_width), jnp.bfloat16),
        pltpu.VMEM(queries.shape, jnp.bfloat16),
        one,
        one,
    ) + (two,) * (chips * heads)
    args = (key_matrix, value_matrix, document.reshape(1, tokens), output_gradient, queries)
    block, query, own, beside, *across = pl.pallas_call(
        functools.partial(prepare_kernel, n_tp, heads),
        out_shape=shapes,
        in_specs=[ANY] * len(args),
        out_specs=(VMEM,) * len(shapes),
        scratch_shapes=[
            pltpu.VMEM((1, tokens), jnp.int32),
            pltpu.SemaphoreType.DMA((2 * heads + 4 + 2 * chips * heads,)),
        ],
        compiler_params=SMALL,
    )(*[pltpu.with_memory_space_constraint(x, pltpu.HBM) for x in args])
    return block, query, own, beside, across


def choose_kernel(at, even_ref, odd_ref, out_ref):
    odd = lax.rem(lax.axis_index("seq"), 2) == 1
    cols = slice(at, at + out_ref.shape[1])

    @pl.when(odd)
    def _():
        out_ref[...] = odd_ref[:, cols]

    @pl.when(jnp.logical_not(odd))
    def _():
        out_ref[...] = even_ref[:, cols]


def choose(even, odd, at=0, width=None):
    shape = (even.shape[0], width or even.shape[1])
    return pl.pallas_call(
        functools.partial(choose_kernel, at),
        out_shape=pltpu.VMEM(shape, even.dtype),
        in_specs=[VMEM, VMEM],
        out_specs=VMEM,
        compiler_params=SMALL,
    )(*held(even, odd))


def lower_kernel(*refs):
    out_ref = refs[-1]
    rows = out_ref.shape[0]
    width = out_ref.shape[1] // (len(refs) - 1)
    for h, ref in enumerate(refs[:-1]):
        out_ref[:, h * width : (h + 1) * width] = ref[rows:, :]


def lower(*pairs):
    rows, width = pairs[0].shape
    return pl.pallas_call(
        lower_kernel,
        out_shape=pltpu.VMEM((rows // 2, width * len(pairs)), pairs[0].dtype),
        in_specs=[VMEM] * len(pairs),
        out_specs=VMEM,
        compiler_params=SMALL,
    )(*held(*pairs))


def relay_kernel(near, *refs):
    total = refs[0][...].astype(jnp.float32)
    for ref in refs[1 : -2 if near else -1]:
        total = total + ref[...].astype(jnp.float32)
    if near:
        odd = lax.rem(lax.axis_index("seq"), 2) == 1
        total = total + jnp.where(odd, refs[-2][...].astype(jnp.float32), 0.0)
    refs[-1][...] = total.astype(refs[-1].dtype)


def relay(near, *parts):
    return pl.pallas_call(
        functools.partial(relay_kernel, near),
        out_shape=pltpu.VMEM(parts[0].shape, jnp.bfloat16),
        in_specs=[VMEM] * len(parts),
        out_specs=VMEM,
        compiler_params=SMALL,
    )(*held(*parts))


def finish_kernel(heads, *refs):
    key_out, value_out = refs[-2:]
    even = lax.rem(lax.axis_index("seq"), 2) == 0
    factor = 1.0 / math.sqrt(HEAD_WIDTH)
    for h in range(heads):
        own, moved, near = refs[3 * h : 3 * h + 3]
        total = own[...] + moved[...].astype(jnp.float32)
        total = total + jnp.where(even, near[...].astype(jnp.float32), 0.0)
        cols = slice(h * HEAD_WIDTH, (h + 1) * HEAD_WIDTH)
        key_out[:, cols] = (total[:, :HEAD_WIDTH] * factor).astype(jnp.bfloat16)
        value_out[:, cols] = total[:, HEAD_WIDTH:].astype(jnp.bfloat16)


def finish(*parts):
    heads = len(parts) // 3
    out = jax.ShapeDtypeStruct((parts[0].shape[0], heads * HEAD_WIDTH), jnp.bfloat16)
    return pl.pallas_call(
        functools.partial(finish_kernel, heads),
        out_shape=(out, out),
        in_specs=[VMEM] * len(parts),
        out_specs=(VMEM, VMEM),
        compiler_params=SMALL,
    )(*held(*parts))


def held(*arrays):
    return [pltpu.with_memory_space_constraint(x, pltpu.VMEM) for x in arrays]


def after(array, *others):
    return lax.optimization_barrier((array, *others))[0]


def nt_dot(a, b):
    return lax.dot_general(a, b, (((1,), (1,)), ((), ())), preferred_element_type=jnp.float32)


def nn_dot(a, b):
    return lax.dot_general(a, b, (((1,), (0,)), ((), ())), preferred_element_type=jnp.float32)


def main_kernel(h, reach, group, n_tp, first, *refs):
    half = reach // 2
    refs = list(refs)
    take = lambda count: [refs.pop(0) for _ in range(count)]
    (query_ref,) = take(1)
    grad_refs = take(n_tp)
    (own_ref,) = take(1)
    odd_refs = take(half)
    even_refs = take(half)
    if not first:
        take(1)
    (dq_ref,) = take(1)
    odd_outs = take(half)
    even_outs = take(half)
    (own_out_ref,) = take(1)
    (kx, vx, kt, qx, gs) = take(5)
    scores, peaks, grads, weights, stats = take(2), take(2), take(2), take(2), take(2)
    (dk_acc, dv_acc, dq_out, out_sems) = take(4)

    T = own_out_ref.shape[0]
    W = group * HEAD_WIDTH
    i = lax.axis_index("seq")
    t = lax.axis_index("tp")
    sub = T // n_tp
    window = (reach + 1) * T
    block_refs = [own_ref]
    for k in range(half):
        block_refs += [odd_refs[k], even_refs[k]]
    dk_acc[...] = jnp.zeros(dk_acc.shape, jnp.float32)
    dv_acc[...] = jnp.zeros(dv_acc.shape, jnp.float32)

    code = lax.broadcasted_iota(jnp.int32, (HEAD_WIDTH, T), 0).astype(jnp.float32)
    for d, block in enumerate(block_refs):
        at = 2 * h * HEAD_WIDTH if block.shape[1] > 2 * HEAD_WIDTH else 0
        row = block[T : T + 1, at : at + T].astype(jnp.float32)
        row = jnp.where(i >= d, row, float(DOCS))
        one_hot = jnp.where(code == row, 1.0, 0.0).astype(jnp.bfloat16)
        rows = slice((reach - d) * T, (reach - d + 1) * T)
        kx[rows, 0:HEAD_WIDTH] = block[0:T, at : at + HEAD_WIDTH]
        kx[rows, HEAD_WIDTH : 2 * HEAD_WIDTH] = one_hot.T
        vx[rows, :] = block[0:T, at + HEAD_WIDTH : at + 2 * HEAD_WIDTH]
    own_row = own_ref[T : T + 1, 0:T].astype(jnp.float32)
    away = jnp.where((code == own_row) | (code > DOCS), 0.0, NEG).astype(jnp.bfloat16).T
    half_rows = T // 2
    for unit in range(group):
        queries_at = slice(unit % 2 * half_rows, (unit % 2 + 1) * half_rows)
        for two in range(2):
            at = (h * group + unit - unit % 2 + two) * HEAD_WIDTH
            rows = slice(two * half_rows, (two + 1) * half_rows)
            qx[unit, rows, 0:HEAD_WIDTH] = query_ref[queries_at, at : at + HEAD_WIDTH]
            qx[unit, rows, HEAD_WIDTH : 2 * HEAD_WIDTH] = away[queries_at, :]

    factor = 1.0 / math.sqrt(HEAD_WIDTH)
    scale = factor * math.log2(math.e)
    seen_rows = window - half_rows
    before = seen_rows - half_rows

    def by_eight(x):
        return x.reshape(x.shape[0] // 8, 8, T)

    def dq_copies(unit, part):
        copies = []
        for two in range(2):
            at = pl.multiple_of((h * group + unit - part + two) * HEAD_WIDTH, HEAD_WIDTH)
            copies.append(
                pltpu.make_async_copy(
                    dq_out.at[unit, pl.ds(two * half_rows, half_rows), :],
                    dq_ref.at[pl.ds(part * half_rows, half_rows), pl.ds(at, HEAD_WIDTH)],
                    out_sems.at[unit, two],
                )
            )
        return copies

    def step(score_of, weight_of, grad_of, b):
        c = 1 - b
        rows = [slice(half_rows * part, half_rows * part + seen_rows) for part in range(2)]
        if score_of is not None:
            s = nt_dot(kx[rows[b], :], qx[score_of])
            query = lax.broadcasted_iota(jnp.int32, (half_rows, T), 1)
            query = jnp.where(query >= half_rows, query - half_rows, query)
            causal = lax.broadcasted_iota(jnp.int32, (half_rows, T), 0) <= query
            own = jnp.where(causal, s[before:], NEG)
            scores[b][0:before] = s[:before]
            scores[b][before:] = own
            peaks[b][...] = jnp.maximum(
                jnp.max(by_eight(s[:before]), axis=0), jnp.max(by_eight(own), axis=0)
            )
        if weight_of is not None:
            top = jnp.max(peaks[c][...], axis=0, keepdims=True) * scale
            dp = nt_dot(vx[rows[c], :], gs[weight_of])
            e = jnp.exp2(scores[c][...] * scale - top)
            weights[c][...] = e.astype(jnp.bfloat16)
            grads[c][...] = dp
            total = jnp.sum(jnp.sum(by_eight(e), axis=0), axis=0, keepdims=True)
            weighted = jnp.sum(jnp.sum(by_eight(e * dp), axis=0), axis=0, keepdims=True)
            stats[c][0:1] = 1.0 / total
            stats[c][1:2] = weighted / total
        if grad_of is not None:
            inverse = stats[b][0:1]
            e_old = weights[b][...]
            ds = (e_old.astype(jnp.float32) * (grads[b][...] - stats[b][1:2])).astype(jnp.bfloat16)
            column = jnp.broadcast_to(inverse, (HEAD_WIDTH, T)).T
            query = (qx[grad_of, :, 0:HEAD_WIDTH].astype(jnp.float32) * column).astype(jnp.bfloat16)
            grad = (gs[grad_of].astype(jnp.float32) * column).astype(jnp.bfloat16)
            dq = nn_dot(kt[:, rows[b]], ds) * (inverse * factor)
            dq_out[grad_of] = dq.T.astype(jnp.bfloat16)
            for copy in dq_copies(grad_of, b):
                copy.start()
            dv_acc[rows[b], :] += nn_dot(e_old, grad)
            dk_acc[rows[b], :] += nn_dot(ds, query)

    def two_steps(pair, _):
        g = 2 * pair
        step(g + 2, g + 1, g, 0)
        step(g + 3, g + 2, g + 1, 1)
        return 0

    step(0, None, None, 0)
    for j in range(reach + 1):
        kt[:, j * T : (j + 1) * T] = kx[j * T : (j + 1) * T, 0:HEAD_WIDTH].T
    for m in range(n_tp):
        first_row = (t ^ m) * sub
        part = first_row // half_rows
        at_row = pl.multiple_of(first_row - part * half_rows, sub)
        for g in range(group):
            at = g * HEAD_WIDTH + (h * W if m < 2 or m % 2 else 0)
            rows = pl.ds(pl.multiple_of(g % 2 * half_rows + at_row, sub), sub)
            gs[g - g % 2 + part, rows, :] = grad_refs[m][0:sub, at : at + HEAD_WIDTH]
    step(1, 0, None, 1)
    lax.fori_loop(0, group // 2 - 1, two_steps, 0)
    step(None, group - 1, group - 2, 0)
    step(None, None, group - 1, 1)

    for d in range(reach + 1):
        dst = (odd_outs if d % 2 else even_outs)[(d - 1) // 2] if d else own_out_ref
        rows = slice((reach - d) * T, (reach - d + 1) * T)
        dst[:, 0:HEAD_WIDTH] = dk_acc[rows, :].astype(dst.dtype)
        dst[:, HEAD_WIDTH : 2 * HEAD_WIDTH] = dv_acc[rows, :].astype(dst.dtype)
    for unit in range(group):
        for copy in dq_copies(unit, unit % 2):
            copy.wait()


def scratch_of(window, T, group):
    bf16, f32 = jnp.bfloat16, jnp.float32
    return [
        pltpu.VMEM((window * T, 2 * HEAD_WIDTH), bf16),
        pltpu.VMEM((window * T, HEAD_WIDTH), bf16),
        pltpu.VMEM((HEAD_WIDTH, window * T), bf16),
        pltpu.VMEM((group, T, 2 * HEAD_WIDTH), bf16),
        pltpu.VMEM((group, T, HEAD_WIDTH), bf16),
        *[pltpu.VMEM((window * T - T // 2, T), f32)] * 2,
        *[pltpu.VMEM((8, T), f32)] * 2,
        *[pltpu.VMEM((window * T - T // 2, T), f32)] * 2,
        *[pltpu.VMEM((window * T - T // 2, T), bf16)] * 2,
        *[pltpu.VMEM((8, T), f32)] * 2,
        pltpu.VMEM((window * T, HEAD_WIDTH), f32),
        pltpu.VMEM((window * T, HEAD_WIDTH), f32),
        pltpu.VMEM((group, T, HEAD_WIDTH), bf16),
    ]


def head_call(h, reach, group, n_tp, queries, grads, block, odds, evens, dq):
    T, q_width = queries.shape
    window = reach + 1
    first = dq is None
    args = held(queries, *grads, block, *odds, *evens)
    specs = [VMEM] * len(args)
    if not first:
        args.append(dq)
        specs.append(ANY)
    flops = 5 * 2 * T * (window * T) * group * HEAD_WIDTH
    scratch = scratch_of(window, T, group)
    outs = pl.pallas_call(
        functools.partial(main_kernel, h, reach, group, n_tp, first),
        out_shape=(pltpu.HBM((T, q_width), jnp.bfloat16),)
        + (pltpu.VMEM((T, 2 * HEAD_WIDTH), jnp.bfloat16),) * reach
        + (pltpu.VMEM((T, 2 * HEAD_WIDTH), jnp.float32),),
        in_specs=specs,
        out_specs=(ANY,) + (VMEM,) * (reach + 1),
        input_output_aliases={} if first else {len(args) - 1: 0},
        scratch_shapes=[*scratch, pltpu.SemaphoreType.DMA((group, 2))],
        compiler_params=pltpu.CompilerParams(
            vmem_limit_bytes=2 * sum(math.prod(x.shape) * x.dtype.itemsize for x in scratch)
        ),
        cost_estimate=pl.CostEstimate(
            flops=4 * flops,
            bytes_accessed=4 * 1024 * 1024,
            transcendentals=T * window * T * group,
        ),
    )(*args)
    half = reach // 2
    return outs[0], outs[1 : half + 1], outs[half + 1 : -1], outs[-1]


def local(queries, key_matrix, value_matrix, output_gradient, document):
    n = lax.axis_size("seq")
    n_tp = lax.axis_size("tp")
    T, q_width = queries.shape
    heads = key_matrix.shape[1] // HEAD_WIDTH
    group = q_width // (heads * HEAD_WIDTH)
    reach = n // 2
    half = reach // 2

    block, queries, mine, beside, across = prepare(
        key_matrix, value_matrix, document, output_gradient, queries, n_tp
    )

    swap = [(a, a ^ 1) for a in range(n)]
    one_up = [(a, (a + 1) % n) for a in range(n)]
    two_up = [(a, (a + 2) % n) for a in range(n)]
    one_down = [(b, a) for a, b in one_up]
    two_down = [(b, a) for a, b in two_up]
    cores = [(a, a ^ 1) for a in range(n_tp)]

    evens = [lax.ppermute(block, "seq", two_up)]
    pairs = [
        lax.ppermute(pair, "tp", [(a, a ^ (2 * (m // heads) + 2)) for a in range(n_tp)])
        for m, pair in enumerate(across)
    ]
    width = 2 * HEAD_WIDTH
    odds = [[None] for _ in range(heads)]
    for k in range(1, half):
        step = choose(evens[-1], evens[-1], 0, width)
        odds[0].append(lax.ppermute(step, "seq", one_up))
        evens.append(lax.ppermute(evens[-1], "seq", two_up))
        for h in range(1, heads):
            step = choose(evens[-2], evens[-2], h * width, width)
            odds[h].append(lax.ppermute(step, "seq", one_up))
    near = lax.ppermute(choose(block, evens[0]), "seq", swap)
    beside = lax.ppermute(beside, "tp", cores)
    grads = [[mine, beside] for _ in range(heads)]
    for m in range(0, len(pairs), heads):
        rest = lax.ppermute(lower(*pairs[m : m + heads]), "tp", cores)
        for h in range(heads):
            grads[h] += [pairs[m + h], rest]

    dq = None
    odds_in, evens_in = [[near, *x[1:]] for x in odds], evens
    leaving = []
    for h in range(heads):
        dq, odds, evens, own = head_call(
            h, reach, group, n_tp, queries, grads[h], block, odds_in[h], evens_in, dq
        )
        last = evens[-1]
        if leaving:
            moved = [*leaving[-1][0], leaving[-1][2]]
            odds = [after(x, *moved) for x in odds]
            last = after(last, *moved)
        moving = lax.ppermute(last, "seq", two_down)
        odds = [lax.ppermute(x, "seq", one_down if k else swap) for k, x in enumerate(odds)]
        leaving.append((odds, evens, moving, own))
    ends = []
    for h in range(heads):
        odds, evens, moving, own = leaving[h]
        for k in range(half - 1, 0, -1):
            if h < heads - 1:
                moving = after(moving, dq)
            parts = [moving, evens[k - 1], odds[k]] + ([odds[0]] if k == 1 else [])
            moving = lax.ppermute(relay(k == 1, *parts), "seq", two_down)
        ends += [own, moving, odds[0]]
    return (dq, *finish(*ends))


def solution(mesh):
    return jax.shard_map(
        local,
        mesh=mesh,
        in_specs=(P("seq", "tp"), P("seq", "tp"), P("seq", "tp"), P(("seq", "tp"), None), P("seq")),
        out_specs=(P("seq", "tp"), P("seq", "tp"), P("seq", "tp")),
        check_vma=False,
    )
```

```python
import functools
import math

import jax
import jax.numpy as jnp
from jax import lax
from jax.experimental import pallas as pl
from jax.experimental.pallas import tpu as pltpu
from jax.sharding import PartitionSpec as P

HEAD_WIDTH = 128
DOCS = 8
PAD = 16
NEG = -1e30
ANY = pl.BlockSpec(memory_space=pl.ANY)
VMEM = pl.BlockSpec(memory_space=pltpu.VMEM)
SMALL = pltpu.CompilerParams(vmem_limit_bytes=2 * 1024 * 1024)


def prepare_kernel(n_tp, heads, key_ref, value_ref, doc_ref, grad_ref, query_ref, *rest):
    outs, (doc_scr, sems) = rest[:-2], rest[-2:]
    block_out, query_out, own_out, beside_out, across_outs = *outs[:4], outs[4:]
    tokens = key_ref.shape[0]
    rows = grad_ref.shape[0]
    me = lax.axis_index("tp")
    width = grad_ref.shape[1] // n_tp
    copies = []

    def add(src, dst):
        copies.append(pltpu.make_async_copy(src, dst, sems.at[len(copies)]))
        copies[-1].start()

    def columns(m, at, size):
        start = pl.multiple_of((me ^ m) * width + at, size)
        return grad_ref.at[:, pl.ds(start, size)]

    add(doc_ref, doc_scr)
    for h in range(heads):
        for part, src in enumerate((key_ref, value_ref)):
            cols = pl.ds((2 * h + part) * HEAD_WIDTH, HEAD_WIDTH)
            add(
                src.at[:, pl.ds(h * HEAD_WIDTH, HEAD_WIDTH)],
                block_out.at[pl.ds(0, tokens), cols],
            )
    part = width // heads
    for m in range(2, n_tp):
        for h in range(heads):
            out = across_outs[(m // 2 - 1) * heads + h]
            src = columns(m, h * part, part)
            add(src, out.at[pl.ds(m % 2 * rows, rows), :])
    add(columns(1, 0, width), beside_out)
    add(columns(0, 0, width), own_out)
    add(query_ref, query_out)
    copies[0].wait()
    row = doc_scr[...].astype(jnp.float32).astype(jnp.bfloat16)
    row = jnp.concatenate([row] * heads, axis=1)
    block_out[tokens : tokens + PAD, :] = jnp.broadcast_to(row, (PAD, row.shape[1]))
    for copy in copies[1:]:
        copy.wait()


def prepare(key_matrix, value_matrix, document, output_gradient, queries, n_tp):
    tokens, kv_width = key_matrix.shape
    heads = kv_width // HEAD_WIDTH
    rows, width = output_gradient.shape
    chips = n_tp // 2 - 1
    one = pltpu.VMEM((rows, width // n_tp), jnp.bfloat16)
    two = pltpu.VMEM((2 * rows, width // n_tp // heads), jnp.bfloat16)
    shapes = (
        pltpu.VMEM((tokens + PAD, 2 * kv_width), jnp.bfloat16),
        pltpu.VMEM(queries.shape, jnp.bfloat16),
        one,
        one,
    ) + (two,) * (chips * heads)
    args = (key_matrix, value_matrix, document.reshape(1, tokens), output_gradient, queries)
    block, query, own, beside, *across = pl.pallas_call(
        functools.partial(prepare_kernel, n_tp, heads),
        out_shape=shapes,
        in_specs=[ANY] * len(args),
        out_specs=(VMEM,) * len(shapes),
        scratch_shapes=[
            pltpu.VMEM((1, tokens), jnp.int32),
            pltpu.SemaphoreType.DMA((2 * heads + 4 + 2 * chips * heads,)),
        ],
        compiler_params=SMALL,
    )(*[pltpu.with_memory_space_constraint(x, pltpu.HBM) for x in args])
    return block, query, own, beside, across


def choose_kernel(at, even_ref, odd_ref, out_ref):
    odd = lax.rem(lax.axis_index("seq"), 2) == 1
    cols = slice(at, at + out_ref.shape[1])

    @pl.when(odd)
    def _():
        out_ref[...] = odd_ref[:, cols]

    @pl.when(jnp.logical_not(odd))
    def _():
        out_ref[...] = even_ref[:, cols]


def choose(even, odd, at=0, width=None):
    shape = (even.shape[0], width or even.shape[1])
    return pl.pallas_call(
        functools.partial(choose_kernel, at),
        out_shape=pltpu.VMEM(shape, even.dtype),
        in_specs=[VMEM, VMEM],
        out_specs=VMEM,
        compiler_params=SMALL,
    )(*held(even, odd))


def lower_kernel(*refs):
    out_ref = refs[-1]
    rows = out_ref.shape[0]
    width = out_ref.shape[1] // (len(refs) - 1)
    for h, ref in enumerate(refs[:-1]):
        out_ref[:, h * width : (h + 1) * width] = ref[rows:, :]


def lower(*pairs):
    rows, width = pairs[0].shape
    return pl.pallas_call(
        lower_kernel,
        out_shape=pltpu.VMEM((rows // 2, width * len(pairs)), pairs[0].dtype),
        in_specs=[VMEM] * len(pairs),
        out_specs=VMEM,
        compiler_params=SMALL,
    )(*held(*pairs))


def relay_kernel(near, *refs):
    total = refs[0][...].astype(jnp.float32)
    for ref in refs[1 : -2 if near else -1]:
        total = total + ref[...].astype(jnp.float32)
    if near:
        odd = lax.rem(lax.axis_index("seq"), 2) == 1
        total = total + jnp.where(odd, refs[-2][...].astype(jnp.float32), 0.0)
    refs[-1][...] = total.astype(refs[-1].dtype)


def relay(near, *parts):
    return pl.pallas_call(
        functools.partial(relay_kernel, near),
        out_shape=pltpu.VMEM(parts[0].shape, jnp.bfloat16),
        in_specs=[VMEM] * len(parts),
        out_specs=VMEM,
        compiler_params=SMALL,
    )(*held(*parts))


def finish_kernel(heads, *refs):
    key_out, value_out = refs[-2:]
    even = lax.rem(lax.axis_index("seq"), 2) == 0
    factor = 1.0 / math.sqrt(HEAD_WIDTH)
    for h in range(heads):
        own, moved, near = refs[3 * h : 3 * h + 3]
        total = own[...] + moved[...].astype(jnp.float32)
        total = total + jnp.where(even, near[...].astype(jnp.float32), 0.0)
        cols = slice(h * HEAD_WIDTH, (h + 1) * HEAD_WIDTH)
        key_out[:, cols] = (total[:, :HEAD_WIDTH] * factor).astype(jnp.bfloat16)
        value_out[:, cols] = total[:, HEAD_WIDTH:].astype(jnp.bfloat16)


def finish(*parts):
    heads = len(parts) // 3
    out = jax.ShapeDtypeStruct((parts[0].shape[0], heads * HEAD_WIDTH), jnp.bfloat16)
    return pl.pallas_call(
        functools.partial(finish_kernel, heads),
        out_shape=(out, out),
        in_specs=[VMEM] * len(parts),
        out_specs=(VMEM, VMEM),
        compiler_params=SMALL,
    )(*held(*parts))


def held(*arrays):
    return [pltpu.with_memory_space_constraint(x, pltpu.VMEM) for x in arrays]


def after(array, *others):
    return lax.optimization_barrier((array, *others))[0]


def nt_dot(a, b):
    return lax.dot_general(a, b, (((1,), (1,)), ((), ())), preferred_element_type=jnp.float32)


def nn_dot(a, b):
    return lax.dot_general(a, b, (((1,), (0,)), ((), ())), preferred_element_type=jnp.float32)


def main_kernel(h, reach, group, n_tp, first, *refs):
    half = reach // 2
    refs = list(refs)
    take = lambda count: [refs.pop(0) for _ in range(count)]
    (query_ref,) = take(1)
    grad_refs = take(n_tp)
    (own_ref,) = take(1)
    odd_refs = take(half)
    even_refs = take(half)
    if not first:
        take(1)
    (dq_ref,) = take(1)
    odd_outs = take(half)
    even_outs = take(half)
    (own_out_ref,) = take(1)
    (kx, vx, kt, qx, gs) = take(5)
    scores, peaks, grads, weights, stats = take(2), take(2), take(2), take(2), take(2)
    (dk_acc, dv_acc, dq_out, out_sems) = take(4)

    T = own_out_ref.shape[0]
    W = group * HEAD_WIDTH
    i = lax.axis_index("seq")
    t = lax.axis_index("tp")
    sub = T // n_tp
    window = (reach + 1) * T
    block_refs = [own_ref]
    for k in range(half):
        block_refs += [odd_refs[k], even_refs[k]]
    dk_acc[...] = jnp.zeros(dk_acc.shape, jnp.float32)
    dv_acc[...] = jnp.zeros(dv_acc.shape, jnp.float32)

    code = lax.broadcasted_iota(jnp.int32, (HEAD_WIDTH, T), 0).astype(jnp.float32)
    for d, block in enumerate(block_refs):
        at = 2 * h * HEAD_WIDTH if block.shape[1] > 2 * HEAD_WIDTH else 0
        row = block[T : T + 1, at : at + T].astype(jnp.float32)
        row = jnp.where(i >= d, row, float(DOCS))
        one_hot = jnp.where(code == row, 1.0, 0.0).astype(jnp.bfloat16)
        rows = slice((reach - d) * T, (reach - d + 1) * T)
        kx[rows, 0:HEAD_WIDTH] = block[0:T, at : at + HEAD_WIDTH]
        kx[rows, HEAD_WIDTH : 2 * HEAD_WIDTH] = one_hot.T
        vx[rows, :] = block[0:T, at + HEAD_WIDTH : at + 2 * HEAD_WIDTH]
    own_row = own_ref[T : T + 1, 0:T].astype(jnp.float32)
    away = jnp.where((code == own_row) | (code > DOCS), 0.0, NEG).astype(jnp.bfloat16).T
    half_rows = T // 2
    for unit in range(group):
        queries_at = slice(unit % 2 * half_rows, (unit % 2 + 1) * half_rows)
        for two in range(2):
            at = (h * group + unit - unit % 2 + two) * HEAD_WIDTH
            rows = slice(two * half_rows, (two + 1) * half_rows)
            qx[unit, rows, 0:HEAD_WIDTH] = query_ref[queries_at, at : at + HEAD_WIDTH]
            qx[unit, rows, HEAD_WIDTH : 2 * HEAD_WIDTH] = away[queries_at, :]

    factor = 1.0 / math.sqrt(HEAD_WIDTH)
    scale = factor * math.log2(math.e)
    seen_rows = window - half_rows
    before = seen_rows - half_rows

    def by_eight(x):
        return x.reshape(x.shape[0] // 8, 8, T)

    def dq_copies(unit, part):
        copies = []
        for two in range(2):
            at = pl.multiple_of((h * group + unit - part + two) * HEAD_WIDTH, HEAD_WIDTH)
            copies.append(
                pltpu.make_async_copy(
                    dq_out.at[unit, pl.ds(two * half_rows, half_rows), :],
                    dq_ref.at[pl.ds(part * half_rows, half_rows), pl.ds(at, HEAD_WIDTH)],
                    out_sems.at[unit, two],
                )
            )
        return copies

    def step(score_of, weight_of, grad_of, b):
        c = 1 - b
        rows = [slice(half_rows * part, half_rows * part + seen_rows) for part in range(2)]
        if score_of is not None:
            s = nt_dot(kx[rows[b], :], qx[score_of])
            query = lax.broadcasted_iota(jnp.int32, (half_rows, T), 1)
            query = jnp.where(query >= half_rows, query - half_rows, query)
            causal = lax.broadcasted_iota(jnp.int32, (half_rows, T), 0) <= query
            own = jnp.where(causal, s[before:], NEG)
            scores[b][0:before] = s[:before]
            scores[b][before:] = own
            peaks[b][...] = jnp.maximum(
                jnp.max(by_eight(s[:before]), axis=0), jnp.max(by_eight(own), axis=0)
            )
        if weight_of is not None:
            top = jnp.max(peaks[c][...], axis=0, keepdims=True) * scale
            dp = nt_dot(vx[rows[c], :], gs[weight_of])
            e = jnp.exp2(scores[c][...] * scale - top)
            weights[c][...] = e.astype(jnp.bfloat16)
            grads[c][...] = dp
            total = jnp.sum(jnp.sum(by_eight(e), axis=0), axis=0, keepdims=True)
            weighted = jnp.sum(jnp.sum(by_eight(e * dp), axis=0), axis=0, keepdims=True)
            stats[c][0:1] = 1.0 / total
            stats[c][1:2] = weighted / total
        if grad_of is not None:
            inverse = stats[b][0:1]
            e_old = weights[b][...]
            ds = (e_old.astype(jnp.float32) * (grads[b][...] - stats[b][1:2])).astype(jnp.bfloat16)
            column = jnp.broadcast_to(inverse, (HEAD_WIDTH, T)).T
            query = (qx[grad_of, :, 0:HEAD_WIDTH].astype(jnp.float32) * column).astype(jnp.bfloat16)
            grad = (gs[grad_of].astype(jnp.float32) * column).astype(jnp.bfloat16)
            dq = nn_dot(kt[:, rows[b]], ds) * (inverse * factor)
            dq_out[grad_of] = dq.T.astype(jnp.bfloat16)
            for copy in dq_copies(grad_of, b):
                copy.start()
            dv_acc[rows[b], :] += nn_dot(e_old, grad)
            dk_acc[rows[b], :] += nn_dot(ds, query)

    def two_steps(pair, _):
        g = 2 * pair
        step(g + 2, g + 1, g, 0)
        step(g + 3, g + 2, g + 1, 1)
        return 0

    step(0, None, None, 0)
    for j in range(reach + 1):
        kt[:, j * T : (j + 1) * T] = kx[j * T : (j + 1) * T, 0:HEAD_WIDTH].T
    for m in range(n_tp):
        first_row = (t ^ m) * sub
        part = first_row // half_rows
        at_row = pl.multiple_of(first_row - part * half_rows, sub)
        for g in range(group):
            at = g * HEAD_WIDTH + (h * W if m < 2 or m % 2 else 0)
            rows = pl.ds(pl.multiple_of(g % 2 * half_rows + at_row, sub), sub)
            gs[g - g % 2 + part, rows, :] = grad_refs[m][0:sub, at : at + HEAD_WIDTH]
    step(1, 0, None, 1)
    lax.fori_loop(0, group // 2 - 1, two_steps, 0)
    step(None, group - 1, group - 2, 0)
    step(None, None, group - 1, 1)

    for d in range(reach + 1):
        dst = (odd_outs if d % 2 else even_outs)[(d - 1) // 2] if d else own_out_ref
        rows = slice((reach - d) * T, (reach - d + 1) * T)
        dst[:, 0:HEAD_WIDTH] = dk_acc[rows, :].astype(dst.dtype)
        dst[:, HEAD_WIDTH : 2 * HEAD_WIDTH] = dv_acc[rows, :].astype(dst.dtype)
    for unit in range(group):
        for copy in dq_copies(unit, unit % 2):
            copy.wait()


def scratch_of(window, T, group):
    bf16, f32 = jnp.bfloat16, jnp.float32
    return [
        pltpu.VMEM((window * T, 2 * HEAD_WIDTH), bf16),
        pltpu.VMEM((window * T, HEAD_WIDTH), bf16),
        pltpu.VMEM((HEAD_WIDTH, window * T), bf16),
        pltpu.VMEM((group, T, 2 * HEAD_WIDTH), bf16),
        pltpu.VMEM((group, T, HEAD_WIDTH), bf16),
        *[pltpu.VMEM((window * T - T // 2, T), f32)] * 2,
        *[pltpu.VMEM((8, T), f32)] * 2,
        *[pltpu.VMEM((window * T - T // 2, T), f32)] * 2,
        *[pltpu.VMEM((window * T - T // 2, T), bf16)] * 2,
        *[pltpu.VMEM((8, T), f32)] * 2,
        pltpu.VMEM((window * T, HEAD_WIDTH), f32),
        pltpu.VMEM((window * T, HEAD_WIDTH), f32),
        pltpu.VMEM((group, T, HEAD_WIDTH), bf16),
    ]


def head_call(h, reach, group, n_tp, queries, grads, block, odds, evens, dq):
    T, q_width = queries.shape
    window = reach + 1
    first = dq is None
    args = held(queries, *grads, block, *odds, *evens)
    specs = [VMEM] * len(args)
    if not first:
        args.append(dq)
        specs.append(ANY)
    flops = 5 * 2 * T * (window * T) * group * HEAD_WIDTH
    scratch = scratch_of(window, T, group)
    outs = pl.pallas_call(
        functools.partial(main_kernel, h, reach, group, n_tp, first),
        out_shape=(pltpu.HBM((T, q_width), jnp.bfloat16),)
        + (pltpu.VMEM((T, 2 * HEAD_WIDTH), jnp.bfloat16),) * reach
        + (pltpu.VMEM((T, 2 * HEAD_WIDTH), jnp.float32),),
        in_specs=specs,
        out_specs=(ANY,) + (VMEM,) * (reach + 1),
        input_output_aliases={} if first else {len(args) - 1: 0},
        scratch_shapes=[*scratch, pltpu.SemaphoreType.DMA((group, 2))],
        compiler_params=pltpu.CompilerParams(
            vmem_limit_bytes=2 * sum(math.prod(x.shape) * x.dtype.itemsize for x in scratch)
        ),
        cost_estimate=pl.CostEstimate(
            flops=4 * flops,
            bytes_accessed=4 * 1024 * 1024,
            transcendentals=T * window * T * group,
        ),
    )(*args)
    half = reach // 2
    return outs[0], outs[1 : half + 1], outs[half + 1 : -1], outs[-1]


def local(queries, key_matrix, value_matrix, output_gradient, document):
    n = lax.axis_size("seq")
    n_tp = lax.axis_size("tp")
    T, q_width = queries.shape
    heads = key_matrix.shape[1] // HEAD_WIDTH
    group = q_width // (heads * HEAD_WIDTH)
    reach = n // 2
    half = reach // 2

    block, queries, mine, beside, across = prepare(
        key_matrix, value_matrix, document, output_gradient, queries, n_tp
    )

    swap = [(a, a ^ 1) for a in range(n)]

    def up(step, low):
        if step == 2:
            return [(a, (a + step) % n) for a in range(n)]
        moved = [(a, a + step) for a in range(low, n - step)]
        unused = [(a, a ^ 1) for a in range(low)]
        return moved + unused + [(n - step + a, low + a) for a in range(step)]

    def down(step, low):
        return [((a + step) % n, a) for a in range(n)]

    cores = [(a, a ^ 1) for a in range(n_tp)]

    evens = [lax.ppermute(block, "seq", up(2, 0))]
    pairs = [
        lax.ppermute(pair, "tp", [(a, a ^ (2 * (m // heads) + 2)) for a in range(n_tp)])
        for m, pair in enumerate(across)
    ]
    width = 2 * HEAD_WIDTH
    odds = [[None] for _ in range(heads)]
    for k in range(1, half):
        step = choose(evens[-1], evens[-1], 0, width)
        odds[0].append(lax.ppermute(step, "seq", up(1, 2 * k)))
        evens.append(lax.ppermute(evens[-1], "seq", up(2, 2 * k)))
        for h in range(1, heads):
            step = choose(evens[-2], evens[-2], h * width, width)
            odds[h].append(lax.ppermute(step, "seq", up(1, 2 * k)))
    near = lax.ppermute(choose(block, evens[0]), "seq", swap)
    beside = lax.ppermute(after(beside, *odds[0][1:]), "tp", cores)
    grads = [[mine, beside] for _ in range(heads)]
    for m in range(0, len(pairs), heads):
        rest = after(lower(*pairs[m : m + heads]), *odds[0][1:])
        rest = lax.ppermute(rest, "tp", cores)
        for h in range(heads):
            grads[h] += [pairs[m + h], rest]

    dq = None
    odds_in, evens_in = [[near, *x[1:]] for x in odds], evens
    leaving = []
    for h in range(heads):
        dq, odds, evens, own = head_call(
            h, reach, group, n_tp, queries, grads[h], block, odds_in[h], evens_in, dq
        )
        last = evens[-1]
        if leaving:
            moved = [*leaving[-1][0], leaving[-1][2]]
            odds = [after(x, *moved) for x in odds]
            last = after(last, *moved)
        moving = lax.ppermute(last, "seq", down(2, 2 * half - 2))
        odds = [
            lax.ppermute(x, "seq", down(1, 2 * k) if k else swap) for k, x in enumerate(odds)
        ]
        leaving.append((odds, evens, moving, own))
    ends = []
    for h in range(heads):
        odds, evens, moving, own = leaving[h]
        for k in range(half - 1, 0, -1):
            if h < heads - 1:
                moving = after(moving, dq)
            parts = [moving, evens[k - 1], odds[k]] + ([odds[0]] if k == 1 else [])
            moving = lax.ppermute(relay(k == 1, *parts), "seq", down(2, 2 * k - 2))
        ends += [own, moving, odds[0]]
    return (dq, *finish(*ends))


def solution(mesh):
    return jax.shard_map(
        local,
        mesh=mesh,
        in_specs=(P("seq", "tp"), P("seq", "tp"), P("seq", "tp"), P(("seq", "tp"), None), P("seq")),
        out_specs=(P("seq", "tp"), P("seq", "tp"), P("seq", "tp")),
        check_vma=False,
    )
```

```python
import functools
import math

import jax
import jax.numpy as jnp
from jax import lax
from jax.experimental import pallas as pl
from jax.experimental.pallas import tpu as pltpu
from jax.sharding import PartitionSpec as P

HEAD_WIDTH = 128
DOCS = 8
PAD = 16
NEG = -1e30
ANY = pl.BlockSpec(memory_space=pl.ANY)
VMEM = pl.BlockSpec(memory_space=pltpu.VMEM)
SMALL = pltpu.CompilerParams(vmem_limit_bytes=2 * 1024 * 1024)


def prepare_kernel(n_tp, heads, key_ref, value_ref, doc_ref, grad_ref, *rest):
    outs, (doc_scr, sems) = rest[:-2], rest[-2:]
    block_out, own_out, beside_out, across_outs = *outs[:3], outs[3:]
    tokens = key_ref.shape[0]
    rows = grad_ref.shape[0]
    me = lax.axis_index("tp")
    width = grad_ref.shape[1] // n_tp
    copies = []

    def add(src, dst):
        copies.append(pltpu.make_async_copy(src, dst, sems.at[len(copies)]))
        copies[-1].start()

    def columns(m, at, size):
        start = pl.multiple_of((me ^ m) * width + at, size)
        return grad_ref.at[:, pl.ds(start, size)]

    add(doc_ref, doc_scr)
    for h in range(heads):
        for part, src in enumerate((key_ref, value_ref)):
            cols = pl.ds((2 * h + part) * HEAD_WIDTH, HEAD_WIDTH)
            add(
                src.at[:, pl.ds(h * HEAD_WIDTH, HEAD_WIDTH)],
                block_out.at[pl.ds(0, tokens), cols],
            )
    part = width // heads
    for m in range(2, n_tp):
        for h in range(heads):
            out = across_outs[(m // 2 - 1) * heads + h]
            src = columns(m, h * part, part)
            add(src, out.at[pl.ds(m % 2 * rows, rows), :])
    add(columns(1, 0, width), beside_out)
    add(columns(0, 0, width), own_out)
    copies[0].wait()
    row = doc_scr[...].astype(jnp.float32).astype(jnp.bfloat16)
    row = jnp.concatenate([row] * heads, axis=1)
    block_out[tokens : tokens + PAD, :] = jnp.broadcast_to(row, (PAD, row.shape[1]))
    for copy in copies[1:]:
        copy.wait()


def prepare(key_matrix, value_matrix, document, output_gradient, n_tp):
    tokens, kv_width = key_matrix.shape
    heads = kv_width // HEAD_WIDTH
    rows, width = output_gradient.shape
    chips = n_tp // 2 - 1
    one = pltpu.VMEM((rows, width // n_tp), jnp.bfloat16)
    two = pltpu.VMEM((2 * rows, width // n_tp // heads), jnp.bfloat16)
    shapes = (
        pltpu.VMEM((tokens + PAD, 2 * kv_width), jnp.bfloat16),
        one,
        one,
    ) + (two,) * (chips * heads)
    args = (key_matrix, value_matrix, document.reshape(1, tokens), output_gradient)
    block, own, beside, *across = pl.pallas_call(
        functools.partial(prepare_kernel, n_tp, heads),
        out_shape=shapes,
        in_specs=[ANY] * len(args),
        out_specs=(VMEM,) * len(shapes),
        scratch_shapes=[
            pltpu.VMEM((1, tokens), jnp.int32),
            pltpu.SemaphoreType.DMA((2 * heads + 4 + 2 * chips * heads,)),
        ],
        compiler_params=SMALL,
    )(*[pltpu.with_memory_space_constraint(x, pltpu.HBM) for x in args])
    return block, own, beside, across


def fetch_kernel(from_ref, out_ref, sem):
    copy = pltpu.make_async_copy(from_ref, out_ref, sem)
    copy.start()
    copy.wait()


def fetch(array):
    return pl.pallas_call(
        fetch_kernel,
        out_shape=pltpu.VMEM(array.shape, array.dtype),
        in_specs=[ANY],
        out_specs=VMEM,
        scratch_shapes=[pltpu.SemaphoreType.DMA],
        compiler_params=SMALL,
    )(pltpu.with_memory_space_constraint(array, pltpu.HBM))


def choose_kernel(at, even_ref, odd_ref, out_ref):
    odd = lax.rem(lax.axis_index("seq"), 2) == 1
    cols = slice(at, at + out_ref.shape[1])

    @pl.when(odd)
    def _():
        out_ref[...] = odd_ref[:, cols]

    @pl.when(jnp.logical_not(odd))
    def _():
        out_ref[...] = even_ref[:, cols]


def choose(even, odd, at=0, width=None):
    shape = (even.shape[0], width or even.shape[1])
    return pl.pallas_call(
        functools.partial(choose_kernel, at),
        out_shape=pltpu.VMEM(shape, even.dtype),
        in_specs=[VMEM, VMEM],
        out_specs=VMEM,
        compiler_params=SMALL,
    )(*held(even, odd))


def lower_kernel(*refs):
    out_ref = refs[-1]
    rows = out_ref.shape[0]
    width = out_ref.shape[1] // (len(refs) - 1)
    for h, ref in enumerate(refs[:-1]):
        out_ref[:, h * width : (h + 1) * width] = ref[rows:, :]


def lower(*pairs):
    rows, width = pairs[0].shape
    return pl.pallas_call(
        lower_kernel,
        out_shape=pltpu.VMEM((rows // 2, width * len(pairs)), pairs[0].dtype),
        in_specs=[VMEM] * len(pairs),
        out_specs=VMEM,
        compiler_params=SMALL,
    )(*held(*pairs))


def relay_kernel(near, *refs):
    total = refs[0][...].astype(jnp.float32)
    for ref in refs[1 : -2 if near else -1]:
        total = total + ref[...].astype(jnp.float32)
    if near:
        odd = lax.rem(lax.axis_index("seq"), 2) == 1
        total = total + jnp.where(odd, refs[-2][...].astype(jnp.float32), 0.0)
    refs[-1][...] = total.astype(refs[-1].dtype)


def relay(near, *parts):
    return pl.pallas_call(
        functools.partial(relay_kernel, near),
        out_shape=pltpu.VMEM(parts[0].shape, jnp.bfloat16),
        in_specs=[VMEM] * len(parts),
        out_specs=VMEM,
        compiler_params=SMALL,
    )(*held(*parts))


def finish_kernel(heads, *refs):
    key_out, value_out = refs[-2:]
    even = lax.rem(lax.axis_index("seq"), 2) == 0
    factor = 1.0 / math.sqrt(HEAD_WIDTH)
    for h in range(heads):
        own, moved, near = refs[3 * h : 3 * h + 3]
        total = own[...] + moved[...].astype(jnp.float32)
        total = total + jnp.where(even, near[...].astype(jnp.float32), 0.0)
        cols = slice(h * HEAD_WIDTH, (h + 1) * HEAD_WIDTH)
        key_out[:, cols] = (total[:, :HEAD_WIDTH] * factor).astype(jnp.bfloat16)
        value_out[:, cols] = total[:, HEAD_WIDTH:].astype(jnp.bfloat16)


def finish(*parts):
    heads = len(parts) // 3
    out = jax.ShapeDtypeStruct((parts[0].shape[0], heads * HEAD_WIDTH), jnp.bfloat16)
    return pl.pallas_call(
        functools.partial(finish_kernel, heads),
        out_shape=(out, out),
        in_specs=[VMEM] * len(parts),
        out_specs=(VMEM, VMEM),
        compiler_params=SMALL,
    )(*held(*parts))


def held(*arrays):
    return [pltpu.with_memory_space_constraint(x, pltpu.VMEM) for x in arrays]


def after(array, *others):
    return lax.optimization_barrier((array, *others))[0]


def nt_dot(a, b):
    return lax.dot_general(a, b, (((1,), (1,)), ((), ())), preferred_element_type=jnp.float32)


def nn_dot(a, b):
    return lax.dot_general(a, b, (((1,), (0,)), ((), ())), preferred_element_type=jnp.float32)


def main_kernel(h, reach, group, n_tp, first, *refs):
    half = reach // 2
    refs = list(refs)
    take = lambda count: [refs.pop(0) for _ in range(count)]
    (query_ref,) = take(1)
    grad_refs = take(n_tp)
    (own_ref,) = take(1)
    odd_refs = take(half)
    even_refs = take(half)
    if not first:
        take(1)
    (dq_ref,) = take(1)
    odd_outs = take(half)
    even_outs = take(half)
    (own_out_ref,) = take(1)
    (kx, vx, kt, qx, gs) = take(5)
    scores, peaks, grads, weights, stats = take(2), take(2), take(2), take(2), take(2)
    (dk_acc, dv_acc, dq_out, out_sems) = take(4)

    T = own_out_ref.shape[0]
    W = group * HEAD_WIDTH
    i = lax.axis_index("seq")
    t = lax.axis_index("tp")
    sub = T // n_tp
    window = (reach + 1) * T
    block_refs = [own_ref]
    for k in range(half):
        block_refs += [odd_refs[k], even_refs[k]]
    dk_acc[...] = jnp.zeros(dk_acc.shape, jnp.float32)
    dv_acc[...] = jnp.zeros(dv_acc.shape, jnp.float32)

    code = lax.broadcasted_iota(jnp.int32, (HEAD_WIDTH, T), 0).astype(jnp.float32)
    for d, block in enumerate(block_refs):
        at = 2 * h * HEAD_WIDTH if block.shape[1] > 2 * HEAD_WIDTH else 0
        row = block[T : T + 1, at : at + T].astype(jnp.float32)
        row = jnp.where(i >= d, row, float(DOCS))
        one_hot = jnp.where(code == row, 1.0, 0.0).astype(jnp.bfloat16)
        rows = slice((reach - d) * T, (reach - d + 1) * T)
        kx[rows, 0:HEAD_WIDTH] = block[0:T, at : at + HEAD_WIDTH]
        kx[rows, HEAD_WIDTH : 2 * HEAD_WIDTH] = one_hot.T
        vx[rows, :] = block[0:T, at + HEAD_WIDTH : at + 2 * HEAD_WIDTH]
    own_row = own_ref[T : T + 1, 0:T].astype(jnp.float32)
    away = jnp.where((code == own_row) | (code > DOCS), 0.0, NEG).astype(jnp.bfloat16).T
    half_rows = T // 2
    for unit in range(group):
        queries_at = slice(unit % 2 * half_rows, (unit % 2 + 1) * half_rows)
        for two in range(2):
            at = (h * group + unit - unit % 2 + two) * HEAD_WIDTH
            rows = slice(two * half_rows, (two + 1) * half_rows)
            qx[unit, rows, 0:HEAD_WIDTH] = query_ref[queries_at, at : at + HEAD_WIDTH]
            qx[unit, rows, HEAD_WIDTH : 2 * HEAD_WIDTH] = away[queries_at, :]

    factor = 1.0 / math.sqrt(HEAD_WIDTH)
    scale = factor * math.log2(math.e)
    seen_rows = window - half_rows
    before = seen_rows - half_rows

    def by_eight(x):
        return x.reshape(x.shape[0] // 8, 8, T)

    def dq_copies(unit, part):
        copies = []
        for two in range(2):
            at = pl.multiple_of((h * group + unit - part + two) * HEAD_WIDTH, HEAD_WIDTH)
            copies.append(
                pltpu.make_async_copy(
                    dq_out.at[unit, pl.ds(two * half_rows, half_rows), :],
                    dq_ref.at[pl.ds(part * half_rows, half_rows), pl.ds(at, HEAD_WIDTH)],
                    out_sems.at[unit, two],
                )
            )
        return copies

    def step(score_of, weight_of, grad_of, b):
        c = 1 - b
        rows = [slice(half_rows * part, half_rows * part + seen_rows) for part in range(2)]
        if score_of is not None:
            s = nt_dot(kx[rows[b], :], qx[score_of])
            query = lax.broadcasted_iota(jnp.int32, (half_rows, T), 1)
            query = jnp.where(query >= half_rows, query - half_rows, query)
            causal = lax.broadcasted_iota(jnp.int32, (half_rows, T), 0) <= query
            own = jnp.where(causal, s[before:], NEG)
            scores[b][0:before] = s[:before]
            scores[b][before:] = own
            peaks[b][...] = jnp.maximum(
                jnp.max(by_eight(s[:before]), axis=0), jnp.max(by_eight(own), axis=0)
            )
        if weight_of is not None:
            top = jnp.max(peaks[c][...], axis=0, keepdims=True) * scale
            dp = nt_dot(vx[rows[c], :], gs[weight_of])
            e = jnp.exp2(scores[c][...] * scale - top)
            weights[c][...] = e.astype(jnp.bfloat16)
            grads[c][...] = dp
            total = jnp.sum(jnp.sum(by_eight(e), axis=0), axis=0, keepdims=True)
            weighted = jnp.sum(jnp.sum(by_eight(e * dp), axis=0), axis=0, keepdims=True)
            stats[c][0:1] = 1.0 / total
            stats[c][1:2] = weighted / total
        if grad_of is not None:
            inverse = stats[b][0:1]
            e_old = weights[b][...]
            ds = (e_old.astype(jnp.float32) * (grads[b][...] - stats[b][1:2])).astype(jnp.bfloat16)
            column = jnp.broadcast_to(inverse, (HEAD_WIDTH, T)).T
            query = (qx[grad_of, :, 0:HEAD_WIDTH].astype(jnp.float32) * column).astype(jnp.bfloat16)
            grad = (gs[grad_of].astype(jnp.float32) * column).astype(jnp.bfloat16)
            dq = nn_dot(kt[:, rows[b]], ds) * (inverse * factor)
            dq_out[grad_of] = dq.T.astype(jnp.bfloat16)
            for copy in dq_copies(grad_of, b):
                copy.start()
            dv_acc[rows[b], :] += nn_dot(e_old, grad)
            dk_acc[rows[b], :] += nn_dot(ds, query)

    def two_steps(pair, _):
        g = 2 * pair
        step(g + 2, g + 1, g, 0)
        step(g + 3, g + 2, g + 1, 1)
        return 0

    step(0, None, None, 0)
    for j in range(reach + 1):
        kt[:, j * T : (j + 1) * T] = kx[j * T : (j + 1) * T, 0:HEAD_WIDTH].T
    for m in range(n_tp):
        first_row = (t ^ m) * sub
        part = first_row // half_rows
        at_row = pl.multiple_of(first_row - part * half_rows, sub)
        for g in range(group):
            at = g * HEAD_WIDTH + (h * W if m < 2 or m % 2 else 0)
            rows = pl.ds(pl.multiple_of(g % 2 * half_rows + at_row, sub), sub)
            gs[g - g % 2 + part, rows, :] = grad_refs[m][0:sub, at : at + HEAD_WIDTH]
    step(1, 0, None, 1)
    lax.fori_loop(0, group // 2 - 1, two_steps, 0)
    step(None, group - 1, group - 2, 0)
    step(None, None, group - 1, 1)

    for d in range(reach + 1):
        dst = (odd_outs if d % 2 else even_outs)[(d - 1) // 2] if d else own_out_ref
        rows = slice((reach - d) * T, (reach - d + 1) * T)
        dst[:, 0:HEAD_WIDTH] = dk_acc[rows, :].astype(dst.dtype)
        dst[:, HEAD_WIDTH : 2 * HEAD_WIDTH] = dv_acc[rows, :].astype(dst.dtype)
    for unit in range(group):
        for copy in dq_copies(unit, unit % 2):
            copy.wait()


def scratch_of(window, T, group):
    bf16, f32 = jnp.bfloat16, jnp.float32
    return [
        pltpu.VMEM((window * T, 2 * HEAD_WIDTH), bf16),
        pltpu.VMEM((window * T, HEAD_WIDTH), bf16),
        pltpu.VMEM((HEAD_WIDTH, window * T), bf16),
        pltpu.VMEM((group, T, 2 * HEAD_WIDTH), bf16),
        pltpu.VMEM((group, T, HEAD_WIDTH), bf16),
        *[pltpu.VMEM((window * T - T // 2, T), f32)] * 2,
        *[pltpu.VMEM((8, T), f32)] * 2,
        *[pltpu.VMEM((window * T - T // 2, T), f32)] * 2,
        *[pltpu.VMEM((window * T - T // 2, T), bf16)] * 2,
        *[pltpu.VMEM((8, T), f32)] * 2,
        pltpu.VMEM((window * T, HEAD_WIDTH), f32),
        pltpu.VMEM((window * T, HEAD_WIDTH), f32),
        pltpu.VMEM((group, T, HEAD_WIDTH), bf16),
    ]


def head_call(h, reach, group, n_tp, queries, grads, block, odds, evens, dq):
    T, q_width = queries.shape
    window = reach + 1
    first = dq is None
    args = held(queries, *grads, block, *odds, *evens)
    specs = [VMEM] * len(args)
    if not first:
        args.append(dq)
        specs.append(ANY)
    flops = 5 * 2 * T * (window * T) * group * HEAD_WIDTH
    scratch = scratch_of(window, T, group)
    outs = pl.pallas_call(
        functools.partial(main_kernel, h, reach, group, n_tp, first),
        out_shape=(pltpu.HBM((T, q_width), jnp.bfloat16),)
        + (pltpu.VMEM((T, 2 * HEAD_WIDTH), jnp.bfloat16),) * reach
        + (pltpu.VMEM((T, 2 * HEAD_WIDTH), jnp.float32),),
        in_specs=specs,
        out_specs=(ANY,) + (VMEM,) * (reach + 1),
        input_output_aliases={} if first else {len(args) - 1: 0},
        scratch_shapes=[*scratch, pltpu.SemaphoreType.DMA((group, 2))],
        compiler_params=pltpu.CompilerParams(
            vmem_limit_bytes=2 * sum(math.prod(x.shape) * x.dtype.itemsize for x in scratch)
        ),
        cost_estimate=pl.CostEstimate(
            flops=4 * flops,
            bytes_accessed=4 * 1024 * 1024,
            transcendentals=T * window * T * group,
        ),
    )(*args)
    half = reach // 2
    return outs[0], outs[1 : half + 1], outs[half + 1 : -1], outs[-1]


def local(queries, key_matrix, value_matrix, output_gradient, document):
    n = lax.axis_size("seq")
    n_tp = lax.axis_size("tp")
    T, q_width = queries.shape
    heads = key_matrix.shape[1] // HEAD_WIDTH
    group = q_width // (heads * HEAD_WIDTH)
    reach = n // 2
    half = reach // 2

    block, mine, beside, across = prepare(
        key_matrix, value_matrix, document, output_gradient, n_tp
    )
    queries = fetch(after(queries, block))

    swap = [(a, a ^ 1) for a in range(n)]

    def up(step, low):
        if step == 2:
            return [(a, (a + step) % n) for a in range(n)]
        moved = [(a, a + step) for a in range(low, n - step)]
        unused = [(a, a ^ 1) for a in range(low)]
        return moved + unused + [(n - step + a, low + a) for a in range(step)]

    def down(step, low):
        return [((a + step) % n, a) for a in range(n)]

    cores = [(a, a ^ 1) for a in range(n_tp)]

    evens = [lax.ppermute(block, "seq", up(2, 0))]
    pairs = [
        lax.ppermute(pair, "tp", [(a, a ^ (2 * (m // heads) + 2)) for a in range(n_tp)])
        for m, pair in enumerate(across)
    ]
    width = 2 * HEAD_WIDTH
    odds = [[None] for _ in range(heads)]
    for k in range(1, half):
        step = choose(evens[-1], evens[-1], 0, width)
        odds[0].append(lax.ppermute(step, "seq", up(1, 2 * k)))
        evens.append(lax.ppermute(evens[-1], "seq", up(2, 2 * k)))
        for h in range(1, heads):
            step = choose(evens[-2], evens[-2], h * width, width)
            odds[h].append(lax.ppermute(step, "seq", up(1, 2 * k)))
    near = lax.ppermute(choose(block, evens[0]), "seq", swap)
    beside = lax.ppermute(after(beside, queries, *odds[0][1:]), "tp", cores)
    grads = [[mine, beside] for _ in range(heads)]
    for m in range(0, len(pairs), heads):
        rest = after(lower(*pairs[m : m + heads]), *odds[0][1:])
        rest = lax.ppermute(rest, "tp", cores)
        for h in range(heads):
            grads[h] += [pairs[m + h], rest]

    dq = None
    odds_in, evens_in = [[near, *x[1:]] for x in odds], evens
    leaving = []
    for h in range(heads):
        dq, odds, evens, own = head_call(
            h, reach, group, n_tp, queries, grads[h], block, odds_in[h], evens_in, dq
        )
        last = evens[-1]
        if leaving:
            moved = [*leaving[-1][0], leaving[-1][2]]
            odds = [after(x, *moved) for x in odds]
            last = after(last, *moved)
        moving = lax.ppermute(last, "seq", down(2, 2 * half - 2))
        odds = [
            lax.ppermute(x, "seq", down(1, 2 * k) if k else swap) for k, x in enumerate(odds)
        ]
        leaving.append((odds, evens, moving, own))
    ends = []
    for h in range(heads):
        odds, evens, moving, own = leaving[h]
        for k in range(half - 1, 0, -1):
            if h < heads - 1:
                moving = after(moving, dq)
            parts = [moving, evens[k - 1], odds[k]] + ([odds[0]] if k == 1 else [])
            moving = lax.ppermute(relay(k == 1, *parts), "seq", down(2, 2 * k - 2))
        ends += [own, moving, odds[0]]
    return (dq, *finish(*ends))


def solution(mesh):
    return jax.shard_map(
        local,
        mesh=mesh,
        in_specs=(P("seq", "tp"), P("seq", "tp"), P("seq", "tp"), P(("seq", "tp"), None), P("seq")),
        out_specs=(P("seq", "tp"), P("seq", "tp"), P("seq", "tp")),
        check_vma=False,
    )
```

```python
import functools
import math

import jax
import jax.numpy as jnp
from jax import lax
from jax.experimental import pallas as pl
from jax.experimental.pallas import tpu as pltpu
from jax.sharding import PartitionSpec as P

HEAD_WIDTH = 128
DOCS = 8
PAD = 16
NEG = -1e30
ANY = pl.BlockSpec(memory_space=pl.ANY)
VMEM = pl.BlockSpec(memory_space=pltpu.VMEM)
SMALL = pltpu.CompilerParams(vmem_limit_bytes=2 * 1024 * 1024)


def prepare_kernel(n_tp, heads, key_ref, value_ref, doc_ref, grad_ref, *rest):
    outs, (doc_scr, sems) = rest[:-2], rest[-2:]
    block_out, across_outs = outs[0], outs[1:]
    tokens = key_ref.shape[0]
    rows = grad_ref.shape[0]
    me = lax.axis_index("tp")
    width = grad_ref.shape[1] // n_tp
    copies = []

    def add(src, dst):
        copies.append(pltpu.make_async_copy(src, dst, sems.at[len(copies)]))
        copies[-1].start()

    def columns(m, at, size):
        start = pl.multiple_of((me ^ m) * width + at, size)
        return grad_ref.at[:, pl.ds(start, size)]

    add(doc_ref, doc_scr)
    for h in range(heads):
        for part, src in enumerate((key_ref, value_ref)):
            cols = pl.ds((2 * h + part) * HEAD_WIDTH, HEAD_WIDTH)
            add(
                src.at[:, pl.ds(h * HEAD_WIDTH, HEAD_WIDTH)],
                block_out.at[pl.ds(0, tokens), cols],
            )
    part = width // heads
    for m in range(2, n_tp):
        for h in range(heads):
            out = across_outs[(m // 2 - 1) * heads + h]
            src = columns(m, h * part, part)
            add(src, out.at[pl.ds(m % 2 * rows, rows), :])
    copies[0].wait()
    row = doc_scr[...].astype(jnp.float32).astype(jnp.bfloat16)
    row = jnp.concatenate([row] * heads, axis=1)
    block_out[tokens : tokens + PAD, :] = jnp.broadcast_to(row, (PAD, row.shape[1]))
    for copy in copies[1:]:
        copy.wait()


def prepare(key_matrix, value_matrix, document, output_gradient, n_tp):
    tokens, kv_width = key_matrix.shape
    heads = kv_width // HEAD_WIDTH
    rows, width = output_gradient.shape
    chips = n_tp // 2 - 1
    two = pltpu.VMEM((2 * rows, width // n_tp // heads), jnp.bfloat16)
    shapes = (
        pltpu.VMEM((tokens + PAD, 2 * kv_width), jnp.bfloat16),
    ) + (two,) * (chips * heads)
    args = (key_matrix, value_matrix, document.reshape(1, tokens), output_gradient)
    block, *across = pl.pallas_call(
        functools.partial(prepare_kernel, n_tp, heads),
        out_shape=shapes,
        in_specs=[ANY] * len(args),
        out_specs=(VMEM,) * len(shapes),
        scratch_shapes=[
            pltpu.VMEM((1, tokens), jnp.int32),
            pltpu.SemaphoreType.DMA((2 * heads + 4 + 2 * chips * heads,)),
        ],
        compiler_params=SMALL,
    )(*[pltpu.with_memory_space_constraint(x, pltpu.HBM) for x in args])
    return block, across


def fetch_kernel(n_tp, query_ref, grad_ref, query_out, own_out, beside_out, sems):
    me = lax.axis_index("tp")
    width = grad_ref.shape[1] // n_tp
    copies = [pltpu.make_async_copy(query_ref, query_out, sems.at[0])]
    for m, out in enumerate((own_out, beside_out)):
        start = pl.multiple_of((me ^ m) * width, width)
        src = grad_ref.at[:, pl.ds(start, width)]
        copies.append(pltpu.make_async_copy(src, out, sems.at[m + 1]))
    for copy in copies:
        copy.start()
    for copy in copies:
        copy.wait()


def fetch(queries, output_gradient, n_tp):
    rows, width = output_gradient.shape
    one = pltpu.VMEM((rows, width // n_tp), jnp.bfloat16)
    args = [pltpu.with_memory_space_constraint(x, pltpu.HBM) for x in (queries, output_gradient)]
    return pl.pallas_call(
        functools.partial(fetch_kernel, n_tp),
        out_shape=(pltpu.VMEM(queries.shape, queries.dtype), one, one),
        in_specs=[ANY, ANY],
        out_specs=(VMEM,) * 3,
        scratch_shapes=[pltpu.SemaphoreType.DMA((3,))],
        compiler_params=SMALL,
    )(*args)


def choose_kernel(at, even_ref, odd_ref, out_ref):
    odd = lax.rem(lax.axis_index("seq"), 2) == 1
    cols = slice(at, at + out_ref.shape[1])

    @pl.when(odd)
    def _():
        out_ref[...] = odd_ref[:, cols]

    @pl.when(jnp.logical_not(odd))
    def _():
        out_ref[...] = even_ref[:, cols]


def choose(even, odd, at=0, width=None):
    shape = (even.shape[0], width or even.shape[1])
    return pl.pallas_call(
        functools.partial(choose_kernel, at),
        out_shape=pltpu.VMEM(shape, even.dtype),
        in_specs=[VMEM, VMEM],
        out_specs=VMEM,
        compiler_params=SMALL,
    )(*held(even, odd))


def lower_kernel(*refs):
    out_ref = refs[-1]
    rows = out_ref.shape[0]
    width = out_ref.shape[1] // (len(refs) - 1)
    for h, ref in enumerate(refs[:-1]):
        out_ref[:, h * width : (h + 1) * width] = ref[rows:, :]


def lower(*pairs):
    rows, width = pairs[0].shape
    return pl.pallas_call(
        lower_kernel,
        out_shape=pltpu.VMEM((rows // 2, width * len(pairs)), pairs[0].dtype),
        in_specs=[VMEM] * len(pairs),
        out_specs=VMEM,
        compiler_params=SMALL,
    )(*held(*pairs))


def relay_kernel(near, *refs):
    total = refs[0][...].astype(jnp.float32)
    for ref in refs[1 : -2 if near else -1]:
        total = total + ref[...].astype(jnp.float32)
    if near:
        odd = lax.rem(lax.axis_index("seq"), 2) == 1
        total = total + jnp.where(odd, refs[-2][...].astype(jnp.float32), 0.0)
    refs[-1][...] = total.astype(refs[-1].dtype)


def relay(near, *parts):
    return pl.pallas_call(
        functools.partial(relay_kernel, near),
        out_shape=pltpu.VMEM(parts[0].shape, jnp.bfloat16),
        in_specs=[VMEM] * len(parts),
        out_specs=VMEM,
        compiler_params=SMALL,
    )(*held(*parts))


def finish_kernel(heads, *refs):
    key_out, value_out = refs[-2:]
    even = lax.rem(lax.axis_index("seq"), 2) == 0
    factor = 1.0 / math.sqrt(HEAD_WIDTH)
    for h in range(heads):
        own, moved, near = refs[3 * h : 3 * h + 3]
        total = own[...] + moved[...].astype(jnp.float32)
        total = total + jnp.where(even, near[...].astype(jnp.float32), 0.0)
        cols = slice(h * HEAD_WIDTH, (h + 1) * HEAD_WIDTH)
        key_out[:, cols] = (total[:, :HEAD_WIDTH] * factor).astype(jnp.bfloat16)
        value_out[:, cols] = total[:, HEAD_WIDTH:].astype(jnp.bfloat16)


def finish(*parts):
    heads = len(parts) // 3
    out = jax.ShapeDtypeStruct((parts[0].shape[0], heads * HEAD_WIDTH), jnp.bfloat16)
    return pl.pallas_call(
        functools.partial(finish_kernel, heads),
        out_shape=(out, out),
        in_specs=[VMEM] * len(parts),
        out_specs=(VMEM, VMEM),
        compiler_params=SMALL,
    )(*held(*parts))


def held(*arrays):
    return [pltpu.with_memory_space_constraint(x, pltpu.VMEM) for x in arrays]


def after(array, *others):
    return lax.optimization_barrier((array, *others))[0]


def nt_dot(a, b):
    return lax.dot_general(a, b, (((1,), (1,)), ((), ())), preferred_element_type=jnp.float32)


def nn_dot(a, b):
    return lax.dot_general(a, b, (((1,), (0,)), ((), ())), preferred_element_type=jnp.float32)


def main_kernel(h, reach, group, n_tp, first, *refs):
    half = reach // 2
    refs = list(refs)
    take = lambda count: [refs.pop(0) for _ in range(count)]
    (query_ref,) = take(1)
    grad_refs = take(n_tp)
    (own_ref,) = take(1)
    odd_refs = take(half)
    even_refs = take(half)
    if not first:
        take(1)
    (dq_ref,) = take(1)
    odd_outs = take(half)
    even_outs = take(half)
    (own_out_ref,) = take(1)
    (kx, vx, kt, qx, gs) = take(5)
    scores, peaks, grads, weights, stats = take(2), take(2), take(2), take(2), take(2)
    (dk_acc, dv_acc, dq_out, out_sems) = take(4)

    T = own_out_ref.shape[0]
    W = group * HEAD_WIDTH
    i = lax.axis_index("seq")
    t = lax.axis_index("tp")
    sub = T // n_tp
    window = (reach + 1) * T
    block_refs = [own_ref]
    for k in range(half):
        block_refs += [odd_refs[k], even_refs[k]]
    dk_acc[...] = jnp.zeros(dk_acc.shape, jnp.float32)
    dv_acc[...] = jnp.zeros(dv_acc.shape, jnp.float32)

    code = lax.broadcasted_iota(jnp.int32, (HEAD_WIDTH, T), 0).astype(jnp.float32)
    for d, block in enumerate(block_refs):
        at = 2 * h * HEAD_WIDTH if block.shape[1] > 2 * HEAD_WIDTH else 0
        row = block[T : T + 1, at : at + T].astype(jnp.float32)
        row = jnp.where(i >= d, row, float(DOCS))
        one_hot = jnp.where(code == row, 1.0, 0.0).astype(jnp.bfloat16)
        rows = slice((reach - d) * T, (reach - d + 1) * T)
        kx[rows, 0:HEAD_WIDTH] = block[0:T, at : at + HEAD_WIDTH]
        kx[rows, HEAD_WIDTH : 2 * HEAD_WIDTH] = one_hot.T
        vx[rows, :] = block[0:T, at + HEAD_WIDTH : at + 2 * HEAD_WIDTH]
    own_row = own_ref[T : T + 1, 0:T].astype(jnp.float32)
    away = jnp.where((code == own_row) | (code > DOCS), 0.0, NEG).astype(jnp.bfloat16).T
    half_rows = T // 2
    for unit in range(group):
        queries_at = slice(unit % 2 * half_rows, (unit % 2 + 1) * half_rows)
        for two in range(2):
            at = (h * group + unit - unit % 2 + two) * HEAD_WIDTH
            rows = slice(two * half_rows, (two + 1) * half_rows)
            qx[unit, rows, 0:HEAD_WIDTH] = query_ref[queries_at, at : at + HEAD_WIDTH]
            qx[unit, rows, HEAD_WIDTH : 2 * HEAD_WIDTH] = away[queries_at, :]

    factor = 1.0 / math.sqrt(HEAD_WIDTH)
    scale = factor * math.log2(math.e)
    seen_rows = window - half_rows
    before = seen_rows - half_rows

    def by_eight(x):
        return x.reshape(x.shape[0] // 8, 8, T)

    def dq_copies(unit, part):
        copies = []
        for two in range(2):
            at = pl.multiple_of((h * group + unit - part + two) * HEAD_WIDTH, HEAD_WIDTH)
            copies.append(
                pltpu.make_async_copy(
                    dq_out.at[unit, pl.ds(two * half_rows, half_rows), :],
                    dq_ref.at[pl.ds(part * half_rows, half_rows), pl.ds(at, HEAD_WIDTH)],
                    out_sems.at[unit, two],
                )
            )
        return copies

    def step(score_of, weight_of, grad_of, b):
        c = 1 - b
        rows = [slice(half_rows * part, half_rows * part + seen_rows) for part in range(2)]
        if score_of is not None:
            s = nt_dot(kx[rows[b], :], qx[score_of])
            query = lax.broadcasted_iota(jnp.int32, (half_rows, T), 1)
            query = jnp.where(query >= half_rows, query - half_rows, query)
            causal = lax.broadcasted_iota(jnp.int32, (half_rows, T), 0) <= query
            own = jnp.where(causal, s[before:], NEG)
            scores[b][0:before] = s[:before]
            scores[b][before:] = own
            peaks[b][...] = jnp.maximum(
                jnp.max(by_eight(s[:before]), axis=0), jnp.max(by_eight(own), axis=0)
            )
        if weight_of is not None:
            top = jnp.max(peaks[c][...], axis=0, keepdims=True) * scale
            dp = nt_dot(vx[rows[c], :], gs[weight_of])
            e = jnp.exp2(scores[c][...] * scale - top)
            weights[c][...] = e.astype(jnp.bfloat16)
            grads[c][...] = dp
            total = jnp.sum(jnp.sum(by_eight(e), axis=0), axis=0, keepdims=True)
            weighted = jnp.sum(jnp.sum(by_eight(e * dp), axis=0), axis=0, keepdims=True)
            stats[c][0:1] = 1.0 / total
            stats[c][1:2] = weighted / total
        if grad_of is not None:
            inverse = stats[b][0:1]
            e_old = weights[b][...]
            ds = (e_old.astype(jnp.float32) * (grads[b][...] - stats[b][1:2])).astype(jnp.bfloat16)
            column = jnp.broadcast_to(inverse, (HEAD_WIDTH, T)).T
            query = (qx[grad_of, :, 0:HEAD_WIDTH].astype(jnp.float32) * column).astype(jnp.bfloat16)
            grad = (gs[grad_of].astype(jnp.float32) * column).astype(jnp.bfloat16)
            dq = nn_dot(kt[:, rows[b]], ds) * (inverse * factor)
            dq_out[grad_of] = dq.T.astype(jnp.bfloat16)
            for copy in dq_copies(grad_of, b):
                copy.start()
            dv_acc[rows[b], :] += nn_dot(e_old, grad)
            dk_acc[rows[b], :] += nn_dot(ds, query)

    def two_steps(pair, _):
        g = 2 * pair
        step(g + 2, g + 1, g, 0)
        step(g + 3, g + 2, g + 1, 1)
        return 0

    step(0, None, None, 0)
    for j in range(reach + 1):
        kt[:, j * T : (j + 1) * T] = kx[j * T : (j + 1) * T, 0:HEAD_WIDTH].T
    for m in range(n_tp):
        first_row = (t ^ m) * sub
        part = first_row // half_rows
        at_row = pl.multiple_of(first_row - part * half_rows, sub)
        for g in range(group):
            at = g * HEAD_WIDTH + (h * W if m < 2 or m % 2 else 0)
            rows = pl.ds(pl.multiple_of(g % 2 * half_rows + at_row, sub), sub)
            gs[g - g % 2 + part, rows, :] = grad_refs[m][0:sub, at : at + HEAD_WIDTH]
    step(1, 0, None, 1)
    lax.fori_loop(0, group // 2 - 1, two_steps, 0)
    step(None, group - 1, group - 2, 0)
    step(None, None, group - 1, 1)

    for d in range(reach + 1):
        dst = (odd_outs if d % 2 else even_outs)[(d - 1) // 2] if d else own_out_ref
        rows = slice((reach - d) * T, (reach - d + 1) * T)
        dst[:, 0:HEAD_WIDTH] = dk_acc[rows, :].astype(dst.dtype)
        dst[:, HEAD_WIDTH : 2 * HEAD_WIDTH] = dv_acc[rows, :].astype(dst.dtype)
    for unit in range(group):
        for copy in dq_copies(unit, unit % 2):
            copy.wait()


def scratch_of(window, T, group):
    bf16, f32 = jnp.bfloat16, jnp.float32
    return [
        pltpu.VMEM((window * T, 2 * HEAD_WIDTH), bf16),
        pltpu.VMEM((window * T, HEAD_WIDTH), bf16),
        pltpu.VMEM((HEAD_WIDTH, window * T), bf16),
        pltpu.VMEM((group, T, 2 * HEAD_WIDTH), bf16),
        pltpu.VMEM((group, T, HEAD_WIDTH), bf16),
        *[pltpu.VMEM((window * T - T // 2, T), f32)] * 2,
        *[pltpu.VMEM((8, T), f32)] * 2,
        *[pltpu.VMEM((window * T - T // 2, T), f32)] * 2,
        *[pltpu.VMEM((window * T - T // 2, T), bf16)] * 2,
        *[pltpu.VMEM((8, T), f32)] * 2,
        pltpu.VMEM((window * T, HEAD_WIDTH), f32),
        pltpu.VMEM((window * T, HEAD_WIDTH), f32),
        pltpu.VMEM((group, T, HEAD_WIDTH), bf16),
    ]


def head_call(h, reach, group, n_tp, queries, grads, block, odds, evens, dq):
    T, q_width = queries.shape
    window = reach + 1
    first = dq is None
    args = held(queries, *grads, block, *odds, *evens)
    specs = [VMEM] * len(args)
    if not first:
        args.append(dq)
        specs.append(ANY)
    flops = 5 * 2 * T * (window * T) * group * HEAD_WIDTH
    scratch = scratch_of(window, T, group)
    outs = pl.pallas_call(
        functools.partial(main_kernel, h, reach, group, n_tp, first),
        out_shape=(pltpu.HBM((T, q_width), jnp.bfloat16),)
        + (pltpu.VMEM((T, 2 * HEAD_WIDTH), jnp.bfloat16),) * reach
        + (pltpu.VMEM((T, 2 * HEAD_WIDTH), jnp.float32),),
        in_specs=specs,
        out_specs=(ANY,) + (VMEM,) * (reach + 1),
        input_output_aliases={} if first else {len(args) - 1: 0},
        scratch_shapes=[*scratch, pltpu.SemaphoreType.DMA((group, 2))],
        compiler_params=pltpu.CompilerParams(
            vmem_limit_bytes=2 * sum(math.prod(x.shape) * x.dtype.itemsize for x in scratch)
        ),
        cost_estimate=pl.CostEstimate(
            flops=4 * flops,
            bytes_accessed=4 * 1024 * 1024,
            transcendentals=T * window * T * group,
        ),
    )(*args)
    half = reach // 2
    return outs[0], outs[1 : half + 1], outs[half + 1 : -1], outs[-1]


def local(queries, key_matrix, value_matrix, output_gradient, document):
    n = lax.axis_size("seq")
    n_tp = lax.axis_size("tp")
    T, q_width = queries.shape
    heads = key_matrix.shape[1] // HEAD_WIDTH
    group = q_width // (heads * HEAD_WIDTH)
    reach = n // 2
    half = reach // 2

    block, across = prepare(
        key_matrix, value_matrix, document, output_gradient, n_tp
    )
    queries, mine, beside = fetch(after(queries, block), output_gradient, n_tp)

    swap = [(a, a ^ 1) for a in range(n)]

    def up(step, low):
        if step == 2:
            return [(a, (a + step) % n) for a in range(n)]
        moved = [(a, a + step) for a in range(low, n - step)]
        unused = [(a, a ^ 1) for a in range(low)]
        return moved + unused + [(n - step + a, low + a) for a in range(step)]

    def down(step, low):
        return [((a + step) % n, a) for a in range(n)]

    cores = [(a, a ^ 1) for a in range(n_tp)]

    evens = [lax.ppermute(block, "seq", up(2, 0))]
    pairs = [
        lax.ppermute(pair, "tp", [(a, a ^ (2 * (m // heads) + 2)) for a in range(n_tp)])
        for m, pair in enumerate(across)
    ]
    width = 2 * HEAD_WIDTH
    odds = [[None] for _ in range(heads)]
    for k in range(1, half):
        step = choose(evens[-1], evens[-1], 0, width)
        odds[0].append(lax.ppermute(step, "seq", up(1, 2 * k)))
        evens.append(lax.ppermute(evens[-1], "seq", up(2, 2 * k)))
        for h in range(1, heads):
            step = choose(evens[-2], evens[-2], h * width, width)
            odds[h].append(lax.ppermute(step, "seq", up(1, 2 * k)))
    near = lax.ppermute(choose(block, evens[0]), "seq", swap)
    beside = lax.ppermute(after(beside, queries, *odds[0][1:]), "tp", cores)
    grads = [[mine, beside] for _ in range(heads)]
    for m in range(0, len(pairs), heads):
        rest = after(lower(*pairs[m : m + heads]), *odds[0][1:])
        rest = lax.ppermute(rest, "tp", cores)
        for h in range(heads):
            grads[h] += [pairs[m + h], rest]

    dq = None
    odds_in, evens_in = [[near, *x[1:]] for x in odds], evens
    leaving = []
    for h in range(heads):
        dq, odds, evens, own = head_call(
            h, reach, group, n_tp, queries, grads[h], block, odds_in[h], evens_in, dq
        )
        last = evens[-1]
        if leaving:
            moved = [*leaving[-1][0], leaving[-1][2]]
            odds = [after(x, *moved) for x in odds]
            last = after(last, *moved)
        moving = lax.ppermute(last, "seq", down(2, 2 * half - 2))
        odds = [
            lax.ppermute(x, "seq", down(1, 2 * k) if k else swap) for k, x in enumerate(odds)
        ]
        leaving.append((odds, evens, moving, own))
    ends = []
    for h in range(heads):
        odds, evens, moving, own = leaving[h]
        for k in range(half - 1, 0, -1):
            if h < heads - 1:
                moving = after(moving, dq)
            parts = [moving, evens[k - 1], odds[k]] + ([odds[0]] if k == 1 else [])
            moving = lax.ppermute(relay(k == 1, *parts), "seq", down(2, 2 * k - 2))
        ends += [own, moving, odds[0]]
    return (dq, *finish(*ends))


def solution(mesh):
    return jax.shard_map(
        local,
        mesh=mesh,
        in_specs=(P("seq", "tp"), P("seq", "tp"), P("seq", "tp"), P(("seq", "tp"), None), P("seq")),
        out_specs=(P("seq", "tp"), P("seq", "tp"), P("seq", "tp")),
        check_vma=False,
    )
```
